128 devices in a mesh: seq: 4 (over y_lo, core), res: 32 (over y_hi, z, x).
Axes of the slice: x: 4, y: 4 (y_hi: 2, y_lo: 2; y = y_hi * 2 + y_lo), z: 4, core: 2. Of those that a mesh axis runs over, the one named last changes fastest.
Arguments:
- lineup_state: bfloat16 [16, 2048, 256], P('seq', 'res'), may hold values from -6 to 6
- couple_state: bfloat16 [2048, 2048, 128], P('seq', 'res'), may hold values from -6 to 6
- lineup_filled: int32 [16, 2048], P('seq', 'res'), may hold values 0 or 1
- observed_amino_flag: int32 [2048], replicated, may hold values 0 or 1
- horizontal_query_matrix: bfloat16 [256, 1024], replicated, may hold values from -0.375 to 0.375
- horizontal_final_matrix: bfloat16 [256, 256], replicated, may hold values from -0.375 to 0.375
- couple_offset_matrix: bfloat16 [128, 8], replicated, as said below
- vertical_query_matrix: bfloat16 [256, 1024], replicated, as said below
- vertical_final_matrix: bfloat16 [256, 256], replicated, may hold values from -0.375 to 0.375
- tensor_mean_side_matrix: bfloat16 [256, 64], replicated, may hold values from -0.375 to 0.375
- tensor_mean_final_matrix: bfloat16 [1024, 128], replicated, may hold values from -0.1875 to 0.1875
Outputs:
- alignment_output: bfloat16 [16, 2048, 256], P('seq', 'res')
- pair_output: bfloat16 [2048, 2048, 128], P('seq', 'res')
The draws below stay inside these ranges and needn't reach their ends.
Inputs may be any that keep to these rules, and one draw needn't show every extreme that they name: `couple_offset_matrix`: pair-bias projection of pair features, one column a head. `vertical_query_matrix`: column attention projections: query, key, value and gate blocks of 256 columns each, heads in order within a block.
All inputs are finite; a program needn't handle non-finite values. No bound on the sum of `lineup_filled` on one device may be relied on, other than what follows from the above.
Results may differ from the reference program's by a relative error of at most 0.038.
The reference program's roundings to bfloat16 on the way count: a program that leaves them out, or rounds other values in their place, can miss the bound.
Values may be sent and summed in bfloat16 or wider, within the bound.
No kernel may reach another device: no remote copies, remote signals or barrier semaphores. Data moves between devices by JAX's collectives and lax.ppermute only.
A program may use at most 128 MiB of HBM per device.

```python
import math
import jax
import jax.numpy as jnp
from jax import lax

LINEUP_FEATURES = 256
PAIR_CHANNELS = 128
FOCUS_GROUPS = 8
GROUP_FEATURES = 32
HIDDEN_FACTORS = 32
HOMOLOG_COUNT = 16
AMINO_COUNT = 2048


def draw_couple_offset_matrix(key, part):
    key = jax.random.fold_in(key, 7)
    random_seed_handle = jax.random.fold_in(key, 0)
    parameter_matrices = jax.random.normal(random_seed_handle, (PAIR_CHANNELS, FOCUS_GROUPS), jnp.float32) / math.sqrt(PAIR_CHANNELS)
    return parameter_matrices.astype(jnp.bfloat16)


def draw_vertical_query_matrix(key, part):
    key = jax.random.fold_in(key, 11)
    random_seed_handle = jax.random.fold_in(key, 0)
    parameter_matrices = jax.random.normal(random_seed_handle, (LINEUP_FEATURES, 4 * FOCUS_GROUPS * GROUP_FEATURES), jnp.float32) / math.sqrt(LINEUP_FEATURES)
    return parameter_matrices.astype(jnp.bfloat16)


def set_ends(array, key, least, high):
    spot = [jax.random.randint(jax.random.fold_in(key, axis), (), 0, length) for axis, length in enumerate(array.shape)]
    longest = array.shape.index(max(array.shape))
    next_to = spot[:longest] + [(spot[longest] + 1) % array.shape[longest]] + spot[longest + 1:]
    return array.at[tuple(spot)].set(least).at[tuple(next_to)].set(high)


def block_levels(key, dims, pieces, low, top_value):
    def one(axis_at, shards_of):
        heights = jax.random.uniform(jax.random.fold_in(jax.random.fold_in(key, 6), axis_at), (shards_of,), jnp.float32, low / len(pieces), top_value / len(pieces))
        return jnp.repeat(jnp.exp(heights), dims[axis_at] // shards_of).reshape((-1,) + (1,) * (len(dims) - axis_at - 1))

    level = one(*pieces[0])
    for cut in pieces[1:]:
        level = level * one(*cut)
    return level


def scatter_about(key, extent, spread, reach, cuts=(), kind=jnp.bfloat16):
    array = spread * jax.random.normal(key, extent, jnp.float32)
    if cuts:
        array = array * block_levels(key, extent, cuts, -0.22, 0.18)
    return jnp.clip(array, -reach, reach).astype(kind)


def setup_inputs(seed: int = 0) -> dict:
    key_of = jax.random.split(jax.random.key(seed), 12)
    return {
        "lineup_state": scatter_about(key_of[0], (HOMOLOG_COUNT, AMINO_COUNT, LINEUP_FEATURES), 1.0, 6.0, ((0, 4), (1, 32))),
        "couple_state": scatter_about(key_of[1], (AMINO_COUNT, AMINO_COUNT, PAIR_CHANNELS), 1.0, 6.0, ((0, 4), (1, 32))),
        "lineup_filled": set_ends((jax.random.randint(key_of[2], (HOMOLOG_COUNT, AMINO_COUNT), 0, 8) < 7).astype(jnp.int32), jax.random.fold_in(key_of[2], 1), 0, 1),
        "observed_amino_flag": set_ends((jax.random.randint(key_of[3], (AMINO_COUNT,), 0, 16) < 15).astype(jnp.int32), jax.random.fold_in(key_of[3], 1), 0, 1),
        "horizontal_query_matrix": scatter_about(key_of[4], (LINEUP_FEATURES, 4 * FOCUS_GROUPS * GROUP_FEATURES), LINEUP_FEATURES ** -0.5, 0.375),
        "horizontal_final_matrix": scatter_about(key_of[5], (FOCUS_GROUPS * GROUP_FEATURES, LINEUP_FEATURES), (FOCUS_GROUPS * GROUP_FEATURES) ** -0.5, 0.375),
        "couple_offset_matrix": draw_couple_offset_matrix(jax.random.fold_in(key_of[11], 71), 0),
        "vertical_query_matrix": draw_vertical_query_matrix(jax.random.fold_in(key_of[11], 71), 0),
        "vertical_final_matrix": scatter_about(key_of[8], (FOCUS_GROUPS * GROUP_FEATURES, LINEUP_FEATURES), (FOCUS_GROUPS * GROUP_FEATURES) ** -0.5, 0.375),
        "tensor_mean_side_matrix": scatter_about(key_of[9], (LINEUP_FEATURES, 2 * HIDDEN_FACTORS), LINEUP_FEATURES ** -0.5, 0.375),
        "tensor_mean_final_matrix": scatter_about(key_of[10], (HIDDEN_FACTORS * HIDDEN_FACTORS, PAIR_CHANNELS), (HIDDEN_FACTORS * HIDDEN_FACTORS) ** -0.5, 0.1875),
    }


def standardize_features(values):
    data = values.astype(jnp.float32)
    centered = data - lax.optimization_barrier(jnp.mean(data, axis=-1, keepdims=True))
    variance = lax.optimization_barrier(jnp.mean(centered * centered, axis=-1, keepdims=True))
    return centered * lax.rsqrt(variance + 1e-05)

def softmax_parts(scores):
    highest = lax.optimization_barrier(jnp.max(scores, axis=-1, keepdims=True))
    expo = jnp.exp(scores - highest)
    parameter_matrices = lax.optimization_barrier(expo.astype(jnp.bfloat16)).astype(jnp.float32)
    return (parameter_matrices, lax.optimization_barrier(jnp.sum(expo, axis=-1)))

def reference(lineup_state, couple_state, lineup_filled, observed_amino_flag, horizontal_query_matrix, horizontal_final_matrix, couple_offset_matrix, vertical_query_matrix, vertical_final_matrix, tensor_mean_side_matrix, tensor_mean_final_matrix):
    feature_span = FOCUS_GROUPS * GROUP_FEATURES
    score_scale = 1.0 / math.sqrt(GROUP_FEATURES)
    present_entries = (lineup_filled * observed_amino_flag[None, :]).astype(jnp.float32)
    block_len = math.gcd(AMINO_COUNT, 64)
    n_blocks = AMINO_COUNT // block_len

    def bias_block(pair_rows):
        standardized_source = standardize_features(pair_rows).astype(jnp.bfloat16)
        flat = jnp.dot(standardized_source.reshape(-1, PAIR_CHANNELS), couple_offset_matrix, preferred_element_type=jnp.float32)
        return flat.reshape(block_len, AMINO_COUNT, FOCUS_GROUPS).astype(jnp.bfloat16)
    bias = lax.map(bias_block, couple_state.reshape(n_blocks, block_len, AMINO_COUNT, PAIR_CHANNELS)).reshape(AMINO_COUNT, AMINO_COUNT, FOCUS_GROUPS)
    bias_heads = bias.astype(jnp.float32).transpose(2, 0, 1)
    standardized_source = standardize_features(lineup_state).astype(jnp.bfloat16)
    linear_map = jnp.dot(standardized_source.reshape(-1, LINEUP_FEATURES), horizontal_query_matrix, preferred_element_type=jnp.float32).reshape(HOMOLOG_COUNT, AMINO_COUNT, 4 * feature_span)
    queries = (linear_map[..., :feature_span] * score_scale).astype(jnp.bfloat16).reshape(HOMOLOG_COUNT, AMINO_COUNT, FOCUS_GROUPS, GROUP_FEATURES)
    key_vals = linear_map[..., feature_span:3 * feature_span].astype(jnp.bfloat16)
    gating = jax.nn.sigmoid(linear_map[..., 3 * feature_span:])

    def row_attend(inputs):
        query_row, kv_row, live_row = inputs
        keys = kv_row[:, :feature_span].reshape(AMINO_COUNT, FOCUS_GROUPS, GROUP_FEATURES).astype(jnp.float32)
        value_row = kv_row[:, feature_span:].reshape(AMINO_COUNT, FOCUS_GROUPS, GROUP_FEATURES).astype(jnp.float32)
        scores = jnp.einsum('qhc,khc->hqk', query_row.astype(jnp.float32), keys) + bias_heads
        scores = jnp.where(live_row[None, None, :] > 0, scores, -1000000000.0)
        parameter_matrices, totals = softmax_parts(scores)
        mixed = jnp.einsum('hqk,khc->qhc', parameter_matrices, value_row) / totals.T[:, :, None]
        return mixed.reshape(AMINO_COUNT, feature_span)
    attended = lax.map(row_attend, (queries, key_vals, present_entries))
    sigmoid_scaled = (gating * attended).astype(jnp.bfloat16)
    horizontal_increment = jnp.dot(sigmoid_scaled.reshape(-1, feature_span), horizontal_final_matrix, preferred_element_type=jnp.float32).reshape(HOMOLOG_COUNT, AMINO_COUNT, LINEUP_FEATURES)
    single_homolog = (lineup_state.astype(jnp.float32) + horizontal_increment).astype(jnp.bfloat16)
    standardized_source = standardize_features(single_homolog).astype(jnp.bfloat16)
    linear_map = jnp.dot(standardized_source.reshape(-1, LINEUP_FEATURES), vertical_query_matrix, preferred_element_type=jnp.float32).reshape(HOMOLOG_COUNT, AMINO_COUNT, 4 * feature_span)
    queries = (linear_map[..., :feature_span] * score_scale).astype(jnp.bfloat16).reshape(HOMOLOG_COUNT, AMINO_COUNT, FOCUS_GROUPS, GROUP_FEATURES)
    keys = linear_map[..., feature_span:2 * feature_span].astype(jnp.bfloat16).reshape(HOMOLOG_COUNT, AMINO_COUNT, FOCUS_GROUPS, GROUP_FEATURES).astype(jnp.float32)
    value_all = linear_map[..., 2 * feature_span:3 * feature_span].astype(jnp.bfloat16).reshape(HOMOLOG_COUNT, AMINO_COUNT, FOCUS_GROUPS, GROUP_FEATURES).astype(jnp.float32)
    gating = jax.nn.sigmoid(linear_map[..., 3 * feature_span:])
    column_entry_mask = lineup_filled.astype(jnp.float32)
    scores = jnp.einsum('qrhc,krhc->rhqk', queries.astype(jnp.float32), keys)
    scores = jnp.where(column_entry_mask.T[:, None, None, :] > 0, scores, -1000000000.0)
    parameter_matrices, totals = softmax_parts(scores)
    mixed = jnp.einsum('rhqk,krhc->qrhc', parameter_matrices, value_all) / totals.transpose(2, 0, 1)[..., None]
    sigmoid_scaled = (gating * mixed.reshape(HOMOLOG_COUNT, AMINO_COUNT, feature_span)).astype(jnp.bfloat16)
    vertical_increment = jnp.dot(sigmoid_scaled.reshape(-1, feature_span), vertical_final_matrix, preferred_element_type=jnp.float32).reshape(HOMOLOG_COUNT, AMINO_COUNT, LINEUP_FEATURES)
    alignment_output = (single_homolog.astype(jnp.float32) + vertical_increment).astype(jnp.bfloat16)
    standardized_source = standardize_features(alignment_output).astype(jnp.bfloat16)
    coupled_result = jnp.dot(standardized_source.reshape(-1, LINEUP_FEATURES), tensor_mean_side_matrix, preferred_element_type=jnp.float32).reshape(HOMOLOG_COUNT, AMINO_COUNT, 2 * HIDDEN_FACTORS)
    coupled_result = (coupled_result * present_entries[..., None]).astype(jnp.bfloat16)
    left = coupled_result[..., :HIDDEN_FACTORS].astype(jnp.float32)
    right = coupled_result[..., HIDDEN_FACTORS:].astype(jnp.float32)
    pair_count = jnp.dot(present_entries.T, present_entries, precision=lax.Precision.HIGHEST)

    def outer_block(inputs):
        left_rows, pair_rows, count_rows = inputs
        outer_sum = jnp.einsum('sic,sjd->ijcd', left_rows, right).reshape(block_len, AMINO_COUNT, HIDDEN_FACTORS * HIDDEN_FACTORS).astype(jnp.bfloat16)
        update = jnp.dot(outer_sum.reshape(-1, HIDDEN_FACTORS * HIDDEN_FACTORS), tensor_mean_final_matrix, preferred_element_type=jnp.float32).reshape(block_len, AMINO_COUNT, PAIR_CHANNELS)
        update = update / jnp.maximum(count_rows, 1.0)[..., None]
        return (pair_rows.astype(jnp.float32) + update).astype(jnp.bfloat16)
    left_blocks = left.reshape(HOMOLOG_COUNT, n_blocks, block_len, HIDDEN_FACTORS).transpose(1, 0, 2, 3)
    pair_output = lax.map(outer_block, (left_blocks, couple_state.reshape(n_blocks, block_len, AMINO_COUNT, PAIR_CHANNELS), pair_count.reshape(n_blocks, block_len, AMINO_COUNT)))
    return (alignment_output, pair_output.reshape(AMINO_COUNT, AMINO_COUNT, PAIR_CHANNELS))
```

```python
import math

import jax
import jax.numpy as jnp
import numpy as np
from jax import lax
from jax.experimental import pallas as pl
from jax.experimental.pallas import tpu as pltpu
from jax.sharding import Mesh, PartitionSpec as P

F32 = jnp.float32
BF16 = jnp.bfloat16

AXES = ("yl", "co", "yh", "zh", "zl", "x")
SIZES = (2, 2, 2, 2, 2, 4)
SEQ = ("yl", "co")
RES = ("yh", "zh", "zl", "x")
SWAPPED = ("yl", "co", "yh", "zh")
COLUMN = ("yh", "zh")
NEAR = ("zl", "x")

SEQS = 4
BLOCK = 64
ROWS = 512
WIDTH = 256
HEADS = 8
HEAD_DIM = 32
ALL_SEQS = 16
OUTER = 32
PAIR = 128
LEFT = ALL_SEQS * OUTER
CHUNK = SEQS * BLOCK + 8
MASKED = -1000000000.0
OTHER = -2000000000.0

NT = (((1,), (1,)), ((), ()))


def swap_pairs():
    pairs = []
    for spot in np.ndindex(2, 2, 2, 2):
        target = (spot[2], spot[3], spot[0], spot[1])
        pairs.append(
            (int(np.ravel_multi_index(spot, (2, 2, 2, 2))), int(np.ravel_multi_index(target, (2, 2, 2, 2))))
        )
    return pairs


def swap(array):
    return lax.ppermute(array, SWAPPED, swap_pairs())


def shift(array, axis, size, step):
    return lax.ppermute(array, axis, [(i, (i + step) % size) for i in range(size)])


def dot(a, b, dims=(((1,), (0,)), ((), ()))):
    return lax.dot_general(a, b, dims, preferred_element_type=F32)


def norm(data):
    centered = data - jnp.mean(data, axis=-1, keepdims=True)
    variance = jnp.mean(centered * centered, axis=-1, keepdims=True)
    return centered * lax.rsqrt(variance + 1e-05)


def iota(shape, dim):
    return lax.broadcasted_iota(jnp.int32, shape, dim)


def pack_body(block_ref, x_ref, filled_ref, flag_ref, out_ref):
    rows = SEQS * BLOCK
    out_ref[:rows, :] = x_ref[...]
    filled = filled_ref[...].astype(F32)
    live = filled * flag_ref[pl.ds(block_ref[0], 1), :].astype(F32)
    lines = [jnp.concatenate([part[i : i + 1] for i in range(SEQS)], axis=1) for part in (filled, live)]
    lines.append(jnp.zeros((6, WIDTH), F32))
    out_ref[rows:, :] = jnp.concatenate(lines, axis=0).astype(BF16)


def pack_chunk(block, lineup_state, lineup_filled, flags):
    vmem = pl.BlockSpec(memory_space=pltpu.VMEM)
    return pl.pallas_call(
        pack_body,
        in_specs=[pl.BlockSpec(memory_space=pltpu.SMEM), vmem, vmem, vmem],
        out_specs=vmem,
        out_shape=jax.ShapeDtypeStruct((CHUNK, WIDTH), BF16),
        name="pack_lineup",
    )(block, lineup_state.reshape(SEQS * BLOCK, WIDTH), lineup_filled, flags.reshape(-1, BLOCK))


GATHERED = 16


def norm_body(x_ref, out_ref, *send_refs):
    rows = SEQS * BLOCK
    normed = norm(x_ref[:rows, :].astype(F32)).astype(BF16)
    for r, part in ((slice(0, rows), normed), (slice(rows, CHUNK), x_ref[rows:, :])):
        out_ref[r, :] = part
        for half, send in enumerate(send_refs):
            for k in range(GATHERED):
                send[k, r, :] = part[:, half * 128 : (half + 1) * 128]


def norm_chunk(chunk):
    send = jax.ShapeDtypeStruct((GATHERED, CHUNK, 128), BF16)
    return pl.pallas_call(
        norm_body,
        out_shape=[jax.ShapeDtypeStruct((CHUNK, WIDTH), BF16), send, send],
        name="norm_lineup",
    )(chunk)


BIAS_STEP = 256
BIAS_PARTS = 2
GROUP = 32
COPIES = 4


def bias_body(pair_ref, weight_ref, out_ref, spread, normed):
    @pl.when(pl.program_id(0) == 0)
    def _():
        wide = weight_ref[...]
        owner = iota((PAIR, WIDTH), 1) // HEADS

        def place(i, carry):
            spread[pl.ds(pl.multiple_of(i * PAIR, PAIR), PAIR), :] = jnp.where(
                owner == i, wide, jnp.zeros_like(wide)
            )
            return carry

        lax.fori_loop(0, GROUP, place, 0)

    groups = BIAS_STEP // GROUP
    cols = BLOCK // BIAS_PARTS
    ones = jnp.ones((PAIR, PAIR), BF16)

    def one(i, carry):
        for g in range(groups):
            raw = pair_ref[g * GROUP + i]
            centered = raw.astype(F32) - dot(raw, ones) * (1.0 / PAIR)
            variance = jnp.mean(centered * centered, axis=-1, keepdims=True)
            normed[g * cols : (g + 1) * cols, pl.ds(pl.multiple_of(i * PAIR, PAIR), PAIR)] = (
                centered * lax.rsqrt(variance + 1e-05)
            ).astype(BF16)
        return carry

    lax.fori_loop(0, GROUP, one, 0, unroll=8)
    result = dot(normed[...], spread[...]).astype(BF16)
    for g in range(groups):
        for c in range(COPIES):
            out_ref[c, g // 2, :, (g % 2) * WIDTH : (g % 2 + 1) * WIDTH] = result[g * cols : (g + 1) * cols]


def bias_blocks(couple_state, couple_offset_matrix, part):
    wide = jnp.tile(couple_offset_matrix, (1, GROUP))
    per_step = BIAS_STEP // BLOCK
    cols = BLOCK // BIAS_PARTS
    return pl.pallas_call(
        bias_body,
        grid=(ROWS // BIAS_STEP,),
        in_specs=[
            pl.BlockSpec((BIAS_STEP, cols, PAIR), lambda i: (i, part, 0)),
            pl.BlockSpec((PAIR, WIDTH), lambda i: (0, 0)),
        ],
        out_specs=pl.BlockSpec((COPIES, per_step, cols, BLOCK * HEADS), lambda i: (0, i, 0, 0)),
        out_shape=jax.ShapeDtypeStruct((COPIES, ROWS // BLOCK, cols, BLOCK * HEADS), BF16),
        scratch_shapes=[
            pltpu.VMEM((GROUP * PAIR, WIDTH), BF16),
            pltpu.VMEM((BIAS_STEP // GROUP * cols, GROUP * PAIR), BF16),
        ],
        compiler_params=pltpu.CompilerParams(vmem_limit_bytes=56 << 20),
        cost_estimate=pl.CostEstimate(flops=8 << 30, bytes_accessed=6 << 20, transcendentals=0),
        name="pair_bias",
    )(couple_state, wide)


KEY_TILE = 256
KEYS = 2048
QH = BLOCK * HEADS


def row_body(
    core_ref, own_ref, x_ref, n0_ref, n1_ref, f0_ref, f1_ref, m0_ref, m1_ref, m2_ref, m3_ref, *refs
):
    bias_refs = refs[:BIAS_PARTS]
    wq_ref, wk_ref, wvt_ref, wg_ref, wo_ref, out_ref, scores, values, live = refs[BIAS_PARTS:]
    s = pl.program_id(0)
    core = core_ref[0]

    @pl.when(s == 0)
    def _():
        out_ref[SEQS * BLOCK :, :] = x_ref[SEQS * BLOCK :, :]
        for side, half, ref in ((0, 0, m0_ref), (0, 1, m1_ref), (1, 0, m2_ref), (1, 1, m3_ref)):
            lanes = ref[...].astype(F32)[:, 1, :]
            live[half * 128 : (half + 1) * 128, side * 128 : side * 128 + 16] = lanes.T

    rows = pl.ds(pl.multiple_of(s * BLOCK, BLOCK), BLOCK)
    mine = own_ref[rows, :]
    queries = (dot(mine, wq_ref[...]) * (1.0 / math.sqrt(HEAD_DIM))).astype(BF16).astype(F32)
    head_rows = (iota((BLOCK, HEADS, WIDTH), 2) // HEAD_DIM) == iota((BLOCK, HEADS, WIDTH), 1)
    spread = (
        jnp.where(head_rows, jnp.broadcast_to(queries[:, None, :], (BLOCK, HEADS, WIDTH)), 0.0)
        .reshape(QH, WIDTH)
        .astype(BF16)
    )
    top = jnp.full((8, QH), -3e38, F32)
    per_tile = KEY_TILE // BLOCK
    cols = BLOCK // BIAS_PARTS
    for side, halves in enumerate(((n0_ref, n1_ref), (f0_ref, f1_ref))):
        owner = core if side == 0 else 1 - core
        mask_rows = live[pl.ds(pl.multiple_of(s * BLOCK, BLOCK), BLOCK), side * 128 : side * 128 + 16]
        for t in range(16 // per_tile):
            first = t * per_tile
            tile = jnp.concatenate(
                [ref[first : first + per_tile].reshape(KEY_TILE, 128) for ref in halves], axis=1
            )
            keys = dot(tile, wk_ref[...]).astype(BF16)
            spot = side * (KEYS // 2) + first * BLOCK
            values[:, spot : spot + KEY_TILE] = dot(wvt_ref[...], tile, NT).astype(BF16)
            start = (first // 8) * 16 + owner * 8 + first % 8
            bias = jnp.concatenate(
                [ref[start + b] for b in range(per_tile) for ref in bias_refs], axis=0
            ).astype(F32)
            product = dot(keys, spread, NT) + bias
            alive = jnp.concatenate(
                [mask_rows[:, first + b : first + b + 1] for b in range(per_tile)], axis=0
            )
            product = jnp.where(alive > 0.0, product, MASKED)
            scores[spot : spot + KEY_TILE, :] = product
            top = jnp.maximum(top, jnp.max(product.reshape(KEY_TILE // 8, 8, QH), axis=0))
    highest = jnp.max(top, axis=0, keepdims=True)
    total = jnp.zeros((8, QH), F32)
    mixed = jnp.zeros((WIDTH, QH), F32)
    for t in range(KEYS // KEY_TILE):
        expo = jnp.exp(scores[t * KEY_TILE : (t + 1) * KEY_TILE, :] - highest)
        total = total + jnp.sum(expo.reshape(KEY_TILE // 8, 8, QH), axis=0)
        mixed = mixed + dot(values[:, t * KEY_TILE : (t + 1) * KEY_TILE], expo.astype(BF16))
    mixed = mixed / jnp.sum(total, axis=0, keepdims=True)
    picked = jnp.where(head_rows, mixed.T.reshape(BLOCK, HEADS, WIDTH), 0.0)
    attended = jnp.sum(picked, axis=1)
    gate = jax.nn.sigmoid(dot(mine, wg_ref[...]))
    added = dot((gate * attended).astype(BF16), wo_ref[...])
    out_ref[rows, :] = (x_ref[rows, :].astype(F32) + added).astype(BF16)


def row_attention(core, own, x, near, far, biases, query_matrix, final_matrix):
    wq, wk, wv, wg = (query_matrix[:, i * WIDTH : (i + 1) * WIDTH] for i in range(4))
    whole = lambda shape: pl.BlockSpec(shape, lambda s: (0,) * len(shape))
    gathered = pl.BlockSpec((GATHERED, BLOCK, 128), lambda s: (0, s, 0))
    masks = pl.BlockSpec((GATHERED, 8, 128), lambda s: (0, SEQS * BLOCK // 8, 0))
    square = whole((WIDTH, WIDTH))
    return pl.pallas_call(
        row_body,
        grid=(SEQS,),
        in_specs=[
            pl.BlockSpec(memory_space=pltpu.SMEM),
            whole((CHUNK, WIDTH)),
            whole((CHUNK, WIDTH)),
            *([gathered] * 4),
            *([masks] * 4),
            *([whole((KEYS // BLOCK, BLOCK // BIAS_PARTS, QH))] * BIAS_PARTS),
            square,
            square,
            square,
            square,
            square,
        ],
        out_specs=whole((CHUNK, WIDTH)),
        out_shape=jax.ShapeDtypeStruct((CHUNK, WIDTH), BF16),
        scratch_shapes=[
            pltpu.VMEM((KEYS, QH), F32),
            pltpu.VMEM((WIDTH, KEYS), BF16),
            pltpu.VMEM((WIDTH, 256), F32),
        ],
        compiler_params=pltpu.CompilerParams(vmem_limit_bytes=48 << 20),
        cost_estimate=pl.CostEstimate(flops=16 << 30, bytes_accessed=8 << 20, transcendentals=4 << 20),
        name="row_attention",
    )(core, own, x, *near, *far, *near, *far, *biases, wq, wk, wv.T, wg, final_matrix)


PART = 16
PART_ROWS = ALL_SEQS * PART
SIDE = LEFT + 128


def column_body(
    mine_ref, x0_ref, x1_ref, x2_ref, x3_ref, w_ref, wo_ref, left_ref, right_ref, out_ref, a_ref, b_ref, masks,
):
    x_refs = (x0_ref, x1_ref, x2_ref, x3_ref)
    mine = mine_ref[0]
    for b in range(4):
        lanes = x_refs[b][SEQS * BLOCK :, :].astype(F32)
        masks[:, b * 128 : b * 128 + 8] = lanes.T
    one_row = iota((PART_ROWS, PART_ROWS), 0)
    one_col = iota((PART_ROWS, PART_ROWS), 1)
    same = (one_row % PART) == (one_col % PART)

    def sequence(shape):
        slot = iota(shape, 0) // PART
        return ((slot // SEQS) ^ mine) * SEQS + slot % SEQS

    keep = iota((PART_ROWS, LEFT), 1) % ALL_SEQS == sequence((PART_ROWS, LEFT))
    keep_flag = iota((PART_ROWS, 128), 1) == sequence((PART_ROWS, 128))
    lane_head = iota((PART_ROWS, WIDTH), 1) // HEAD_DIM
    for g in range(BLOCK // PART):
        spots = [(s // SEQS, (s % SEQS) * BLOCK + g * PART) for s in range(ALL_SEQS)]
        data = jnp.concatenate([x_refs[b][r : r + PART, :] for b, r in spots], axis=0).astype(F32)
        filled = jnp.concatenate([masks[r : r + PART, b * 128 : b * 128 + 1] for b, r in spots], axis=0)
        live = jnp.concatenate([masks[r : r + PART, b * 128 + 1 : b * 128 + 2] for b, r in spots], axis=0)
        filled_lane = jnp.broadcast_to(filled, (PART_ROWS, 128)).T[0:1, :]
        fill = jnp.where(same, MASKED, OTHER)
        use = jnp.logical_and(same, jnp.broadcast_to(filled_lane, (PART_ROWS, PART_ROWS)) > 0.0)
        line = dot(norm(data).astype(BF16), w_ref[...])
        queries = (line[:, :WIDTH] * (1.0 / math.sqrt(HEAD_DIM))).astype(BF16)
        keys = line[:, WIDTH : 2 * WIDTH].astype(BF16)
        value = line[:, 2 * WIDTH : 3 * WIDTH].astype(BF16)
        gate = jax.nn.sigmoid(line[:, 3 * WIDTH :])
        mixed = jnp.zeros((PART_ROWS, WIDTH), F32)
        for h in range(HEADS):
            head = lane_head == h
            product = dot(jnp.where(head, queries, jnp.zeros_like(queries)), keys, NT)
            product = jnp.where(use, product, fill)
            expo = jnp.exp(product - jnp.max(product, axis=1, keepdims=True))
            total = jnp.sum(expo, axis=1, keepdims=True)
            mixed = mixed + jnp.where(head, dot(expo.astype(BF16), value) / total, 0.0)
        result = (data + dot((gate * mixed).astype(BF16), wo_ref[...])).astype(BF16)
        for s in range(SEQS):
            out_ref[s * BLOCK + g * PART : s * BLOCK + (g + 1) * PART, :] = result[s * PART : (s + 1) * PART]
        normed = norm(result.astype(F32)).astype(BF16)
        flags = jnp.where(keep_flag, jnp.broadcast_to(live, (PART_ROWS, 128)), 0.0)
        flags = jnp.sum(flags.reshape(ALL_SEQS, PART, 128), axis=0).astype(BF16)
        for weight_ref, out in ((left_ref, a_ref), (right_ref, b_ref)):
            wide = (dot(normed, weight_ref[...]) * live).astype(BF16).astype(F32)
            wide = jnp.where(keep, wide, 0.0)
            wide = jnp.sum(wide.reshape(ALL_SEQS, PART, LEFT), axis=0).astype(BF16)
            for k in range(out.shape[0]):
                out[k, g * PART : (g + 1) * PART, :LEFT] = wide
                out[k, g * PART : (g + 1) * PART, LEFT:] = flags


def column_attention(mine, rows, query_matrix, final_matrix, side_matrix):
    left = jnp.repeat(side_matrix[:, :OUTER], ALL_SEQS, axis=1)
    right = jnp.repeat(side_matrix[:, OUTER:], ALL_SEQS, axis=1)
    vmem = pl.BlockSpec(memory_space=pltpu.VMEM)
    return pl.pallas_call(
        column_body,
        in_specs=[pl.BlockSpec(memory_space=pltpu.SMEM)] + [vmem] * 8,
        out_specs=[vmem] * 3,
        out_shape=[
            jax.ShapeDtypeStruct((SEQS * BLOCK, WIDTH), BF16),
            jax.ShapeDtypeStruct((8, BLOCK, SIDE), BF16),
            jax.ShapeDtypeStruct((1, BLOCK, SIDE), BF16),
        ],
        scratch_shapes=[pltpu.VMEM((WIDTH, 512), F32)],
        compiler_params=pltpu.CompilerParams(vmem_limit_bytes=48 << 20),
        cost_estimate=pl.CostEstimate(flops=4 << 30, bytes_accessed=3 << 20, transcendentals=2 << 20),
        name="column_attention",
    )(mine, *rows, query_matrix, final_matrix, left, right)


PAIR_STEP = 128
WIDE = BLOCK * PAIR
STRIDE = BLOCK + 8


def pair_body(a_ref, b_ref, w_ref, pair_ref, out_ref, table, update):
    @pl.when(pl.program_id(0) == 0)
    def _():
        keep = (iota((16 * ALL_SEQS, LEFT), 1) % ALL_SEQS) == (iota((16 * ALL_SEQS, LEFT), 0) % ALL_SEQS)
        fold = (iota((LEFT, 128), 0) // ALL_SEQS == iota((LEFT, 128), 1)).astype(BF16)

        def build(q, carry):
            rows = b_ref[pl.ds(pl.multiple_of(q * 16, 16), 16), :LEFT].astype(F32)
            rows = jnp.broadcast_to(rows[:, None, :], (16, ALL_SEQS, LEFT)).reshape(16 * ALL_SEQS, LEFT)
            right = dot(jnp.where(keep, rows, 0.0).astype(BF16), fold).astype(BF16)
            for c in range(OUTER // 2):
                part = dot(right, w_ref[:, c * 256 : (c + 1) * 256]).astype(BF16)
                for j in range(16):
                    lanes = pl.ds(pl.multiple_of((q * 16 + j) * PAIR, PAIR), PAIR)
                    for d in range(2):
                        table[(2 * c + d) * 16 : (2 * c + d + 1) * 16, lanes] = part[
                            j * 16 : (j + 1) * 16, d * PAIR : (d + 1) * PAIR
                        ]
            return carry

        lax.fori_loop(0, BLOCK // 16, build, 0)

    left = a_ref[:, :LEFT]
    count = dot(a_ref[:, LEFT:], b_ref[:, LEFT:], NT)
    scale = 1.0 / jnp.maximum(count, 1.0)
    per_dot = 4
    for j in range(0, BLOCK, per_dot):
        part = dot(left, table[:, j * PAIR : (j + per_dot) * PAIR])
        for d in range(per_dot):
            update[pl.ds(j + d, PAIR_STEP, stride=STRIDE), :] = (
                part[:, d * PAIR : (d + 1) * PAIR] * scale[:, j + d : j + d + 1]
            )

    def finish(i, carry):
        rows = update[pl.ds(pl.multiple_of(i * STRIDE, 8), BLOCK), :]
        out_ref[i] = (pair_ref[i].astype(F32) + rows).astype(BF16)
        return carry

    lax.fori_loop(0, PAIR_STEP, finish, 0, unroll=4)


def pair_update(left, right, final_matrix, couple_state):
    wide = final_matrix.reshape(OUTER, OUTER, PAIR).transpose(1, 0, 2).reshape(OUTER, OUTER * PAIR)
    wide = jnp.pad(wide, ((0, 128 - OUTER), (0, 0)))
    block = pl.BlockSpec((PAIR_STEP, BLOCK, PAIR), lambda i: (i, 0, 0))
    return pl.pallas_call(
        pair_body,
        grid=(ROWS // PAIR_STEP,),
        in_specs=[
            pl.BlockSpec((PAIR_STEP, SIDE), lambda i: (i, 0)),
            pl.BlockSpec((BLOCK, SIDE), lambda i: (0, 0)),
            pl.BlockSpec((128, OUTER * PAIR), lambda i: (0, 0)),
            block,
        ],
        out_specs=block,
        out_shape=jax.ShapeDtypeStruct(couple_state.shape, BF16),
        scratch_shapes=[
            pltpu.VMEM((LEFT, WIDE), BF16),
            pltpu.VMEM((STRIDE * PAIR_STEP, PAIR), F32),
        ],
        compiler_params=pltpu.CompilerParams(vmem_limit_bytes=56 << 20),
        cost_estimate=pl.CostEstimate(flops=8 << 30, bytes_accessed=18 << 20, transcendentals=0),
        name="pair_update",
    )(left, right, wide, couple_state)


def per_device(
    lineup_state,
    couple_state,
    lineup_filled,
    observed_amino_flag,
    horizontal_query_matrix,
    horizontal_final_matrix,
    couple_offset_matrix,
    vertical_query_matrix,
    vertical_final_matrix,
    tensor_mean_side_matrix,
    tensor_mean_final_matrix,
):
    core = lax.axis_index("co").astype(jnp.int32).reshape(1)
    block = lax.axis_index(RES).astype(jnp.int32).reshape(1)
    mine = (lax.axis_index("yh") * 2 + lax.axis_index("zh")).astype(jnp.int32).reshape(1)
    chunk = swap(pack_chunk(block, lineup_state, lineup_filled, observed_amino_flag))
    normed, *sends = norm_chunk(chunk)
    near = [lax.all_to_all(send, ("yl", "zl", "x"), 0, 0) for send in sends]
    far = [lax.ppermute(part, "co", [(0, 1), (1, 0)]) for part in near]
    biases = []
    for part in range(BIAS_PARTS):
        send = bias_blocks(couple_state, couple_offset_matrix, part)
        send = send.reshape((32,) + send.shape[2:])
        biases.append(lax.all_to_all(send, RES, 0, 0))
    rows = row_attention(
        core, normed, chunk, near, far, biases, horizontal_query_matrix, horizontal_final_matrix
    )
    rows = [rows] + [lax.ppermute(rows, COLUMN, [(i, i ^ k) for i in range(4)]) for k in (1, 2, 3)]
    aligned, left, right = column_attention(
        mine, rows, vertical_query_matrix, vertical_final_matrix, tensor_mean_side_matrix
    )
    right = swap(right[0])
    aligned = swap(aligned)
    left = lax.all_to_all(left, NEAR, 0, 0)
    pair = pair_update(left.reshape(ROWS, SIDE), right, tensor_mean_final_matrix, couple_state)
    return aligned.reshape(SEQS, BLOCK, WIDTH), pair


def solution(mesh):
    fine = Mesh(mesh.devices.reshape(SIZES), AXES)
    return jax.shard_map(
        per_device,
        mesh=fine,
        in_specs=(
            P(SEQ, RES, None),
            P(SEQ, RES, None),
            P(SEQ, RES),
            P(),
            P(),
            P(),
            P(),
            P(),
            P(),
            P(),
            P(),
        ),
        out_specs=(P(SEQ, RES, None), P(SEQ, RES, None)),
        check_vma=False,
    )
```

```python
import itertools
import math

import jax
import jax.numpy as jnp
import numpy as np
from jax import lax
from jax.experimental import pallas as pl
from jax.experimental.pallas import tpu as pltpu
from jax.sharding import Mesh, PartitionSpec as P

F32 = jnp.float32
BF16 = jnp.bfloat16

AXES = ("yl", "co", "yh", "zh", "zl", "x")
SIZES = (2, 2, 2, 2, 2, 4)
SEQ = ("yl", "co")
RES = ("yh", "zh", "zl", "x")
SWAPPED = ("yl", "co", "yh", "zh")
COLUMN = ("yh", "zh")
NEAR = ("zl", "x")

SEQS = 4
BLOCK = 64
ROWS = 512
WIDTH = 256
HEADS = 8
HEAD_DIM = 32
ALL_SEQS = 16
OUTER = 32
PAIR = 128
LEFT = ALL_SEQS * OUTER
CHUNK = SEQS * BLOCK + 8
MASKED = -1000000000.0
OTHER = -2000000000.0

FLIP = [(0, 1), (1, 0)]
NT = (((1,), (1,)), ((), ()))


def swap_pairs(flip):
    pairs = []
    for spot in np.ndindex(2, 2, 2, 2):
        target = (spot[2] ^ flip, spot[3], spot[0], spot[1])
        pairs.append(
            (int(np.ravel_multi_index(spot, (2, 2, 2, 2))), int(np.ravel_multi_index(target, (2, 2, 2, 2))))
        )
    return pairs


def swap(array, flip=0):
    return lax.ppermute(array, SWAPPED, swap_pairs(flip))


def shift(array, step, flip=0):
    return lax.ppermute(array, NEAR, [(z * 4 + i, (z ^ flip) * 4 + (i + step) % 4) for z in (0, 1) for i in range(4)])


def tie_body(*refs):
    pass


def tie(array, *first):
    anywhere = pl.BlockSpec(memory_space=pl.ANY)
    return pl.pallas_call(
        tie_body,
        in_specs=[anywhere] * (1 + len(first)),
        out_specs=anywhere,
        out_shape=jax.ShapeDtypeStruct(array.shape, array.dtype),
        input_output_aliases={0: 0},
        name="tie",
    )(array, *first)


def dot(a, b, dims=(((1,), (0,)), ((), ()))):
    return lax.dot_general(a, b, dims, preferred_element_type=F32)


def norm(data):
    centered = data - jnp.mean(data, axis=-1, keepdims=True)
    variance = jnp.mean(centered * centered, axis=-1, keepdims=True)
    return centered * lax.rsqrt(variance + 1e-05)


def iota(shape, dim):
    return lax.broadcasted_iota(jnp.int32, shape, dim)


def pack_body(block_ref, x_ref, filled_ref, flag_ref, out_ref):
    rows = SEQS * BLOCK
    out_ref[:rows, :] = x_ref[...]
    filled = filled_ref[...].astype(F32)
    block = block_ref[0]
    flags = flag_ref[pl.ds(block // 2, 1), :].astype(F32)
    live = filled * jnp.where(block % 2 == 0, flags[:, :BLOCK], flags[:, BLOCK:])
    lines = [jnp.concatenate([part[i : i + 1] for i in range(SEQS)], axis=1) for part in (filled, live)]
    lines.append(jnp.zeros((6, WIDTH), F32))
    out_ref[rows:, :] = jnp.concatenate(lines, axis=0).astype(BF16)


def pack_chunk(block, lineup_state, lineup_filled, flags):
    vmem = pl.BlockSpec(memory_space=pltpu.VMEM)
    return pl.pallas_call(
        pack_body,
        in_specs=[pl.BlockSpec(memory_space=pltpu.SMEM), vmem, vmem, vmem],
        out_specs=vmem,
        out_shape=jax.ShapeDtypeStruct((CHUNK, WIDTH), BF16),
        name="pack_lineup",
    )(block, lineup_state.reshape(SEQS * BLOCK, WIDTH), lineup_filled, flags.reshape(-1, 2 * BLOCK))


def norm_body(x_ref, flipped_ref, after_ref, out_ref):
    rows = SEQS * BLOCK
    for slot, ref in enumerate((x_ref, flipped_ref)):
        out_ref[slot, :rows, :] = norm(ref[:rows, :].astype(F32)).astype(BF16)
        out_ref[slot, rows:, :] = ref[rows:, :]


def norm_chunks(chunk, flipped, after):
    vmem = pl.BlockSpec(memory_space=pltpu.VMEM)
    return pl.pallas_call(
        norm_body,
        in_specs=[vmem, vmem, pl.BlockSpec(memory_space=pl.ANY)],
        out_shape=jax.ShapeDtypeStruct((2, CHUNK, WIDTH), BF16),
        name="norm_lineup",
    )(chunk, flipped, after)


BIAS_STEP = 128
BIAS_PARTS = 1
GROUP = 32
COPIES = 4


def bias_body(pair_ref, weight_ref, *refs):
    out_ref, spread, normed = refs[-3:]

    @pl.when(pl.program_id(0) == 0)
    def _():
        wide = weight_ref[...]
        owner = iota((PAIR, WIDTH), 1) // HEADS

        def place(i, carry):
            spread[pl.ds(pl.multiple_of(i * PAIR, PAIR), PAIR), :] = jnp.where(
                owner == i, wide, jnp.zeros_like(wide)
            )
            return carry

        lax.fori_loop(0, GROUP, place, 0)

    groups = BIAS_STEP // GROUP
    cols = BLOCK // BIAS_PARTS
    ones = jnp.ones((PAIR, PAIR), BF16)

    def one(i, carry):
        for g in range(groups):
            raw = pair_ref[g * GROUP + i]
            centered = raw.astype(F32) - dot(raw, ones) * (1.0 / PAIR)
            variance = jnp.mean(centered * centered, axis=-1, keepdims=True)
            normed[g * cols : (g + 1) * cols, pl.ds(pl.multiple_of(i * PAIR, PAIR), PAIR)] = (
                centered * lax.rsqrt(variance + 1e-05)
            ).astype(BF16)
        return carry

    lax.fori_loop(0, GROUP, one, 0, unroll=8)
    result = dot(normed[...], spread[...]).astype(BF16)
    for g in range(groups):
        for c in range(COPIES):
            out_ref[c, g // 2, :, (g % 2) * WIDTH : (g % 2 + 1) * WIDTH] = result[g * cols : (g + 1) * cols]


def bias_blocks(couple_state, couple_offset_matrix, start, steps, *after):
    wide = jnp.tile(couple_offset_matrix, (1, GROUP))
    per_step = BIAS_STEP // BLOCK
    cols = BLOCK // BIAS_PARTS
    return pl.pallas_call(
        bias_body,
        grid=(steps,),
        in_specs=[
            pl.BlockSpec((BIAS_STEP, cols, PAIR), lambda i: (i + start, 0, 0)),
            pl.BlockSpec((PAIR, WIDTH), lambda i: (0, 0)),
        ]
        + [pl.BlockSpec(memory_space=pl.ANY)] * len(after),
        out_specs=pl.BlockSpec((COPIES, per_step, cols, BLOCK * HEADS), lambda i: (0, i + start, 0, 0)),
        out_shape=jax.ShapeDtypeStruct((COPIES, ROWS // BLOCK, cols, BLOCK * HEADS), BF16),
        scratch_shapes=[
            pltpu.VMEM((GROUP * PAIR, WIDTH), BF16),
            pltpu.VMEM((BIAS_STEP // GROUP * cols, GROUP * PAIR), BF16),
        ],
        compiler_params=pltpu.CompilerParams(vmem_limit_bytes=53 << 20),
        cost_estimate=pl.CostEstimate(flops=8 << 30, bytes_accessed=6 << 20, transcendentals=0),
        input_output_aliases={2: 0} if start else {},
        name="pair_bias",
    )(couple_state, wide, *after)


KEY_TILE = 512
KEYS = 2048
QH = BLOCK * HEADS
PER_TILE = KEY_TILE // BLOCK
SPOTS = [(zl, x, co) for co in (0, 1) for zl in (0, 1) for x in (0, 1, 3, 2)]


def key_body(*refs):
    parts, flags = refs[: len(SPOTS)], refs[len(SPOTS) : 2 * len(SPOTS)]
    wk_ref, wvt_ref, key_ref, value_ref, live_ref = refs[2 * len(SPOTS) :]

    @pl.when(pl.program_id(0) == 0)
    def _():
        lanes = jnp.concatenate([ref[...].astype(F32)[:, 1, :] for ref in flags], axis=0)
        live_ref[...] = jnp.concatenate([lanes, jnp.zeros((128 - 2 * len(SPOTS), WIDTH), F32)], axis=0).T

    for t in range(KEYS // KEY_TILE):
        blocks = [(b // 2, b % 2) for b in range(t * PER_TILE, (t + 1) * PER_TILE)]
        tile = jnp.concatenate([parts[i][slot] for i, slot in blocks], axis=0)
        lanes = slice(t * KEY_TILE, (t + 1) * KEY_TILE)
        key_ref[0, lanes, :] = dot(tile, wk_ref[...]).astype(BF16)
        value_ref[0, :, lanes] = dot(wvt_ref[...], tile, NT).astype(BF16)


def row_keys(parts, wk, wv):
    gathered = pl.BlockSpec((2, BLOCK, WIDTH), lambda s: (0, s, 0))
    masks = pl.BlockSpec((2, 8, WIDTH), lambda s: (0, SEQS * BLOCK // 8, 0))
    square = pl.BlockSpec((WIDTH, WIDTH), lambda s: (0, 0))
    return pl.pallas_call(
        key_body,
        grid=(SEQS,),
        in_specs=[*([gathered] * len(SPOTS)), *([masks] * len(SPOTS)), square, square],
        out_specs=[
            pl.BlockSpec((1, KEYS, WIDTH), lambda s: (s, 0, 0)),
            pl.BlockSpec((1, WIDTH, KEYS), lambda s: (s, 0, 0)),
            pl.BlockSpec((WIDTH, 128), lambda s: (0, 0)),
        ],
        out_shape=[
            jax.ShapeDtypeStruct((SEQS, KEYS, WIDTH), BF16),
            jax.ShapeDtypeStruct((SEQS, WIDTH, KEYS), BF16),
            jax.ShapeDtypeStruct((WIDTH, 128), F32),
        ],
        compiler_params=pltpu.CompilerParams(vmem_limit_bytes=57 << 20),
        cost_estimate=pl.CostEstimate(flops=4 << 30, bytes_accessed=12 << 20, transcendentals=0),
        name="row_keys",
    )(*parts, *parts, wk, wv.T)


def row_body(spot_ref, own_ref, x_ref, key_ref, value_ref, live, *refs):
    bias_refs = refs[:BIAS_PARTS]
    wq_ref, wg_ref, wo_ref, out_ref, *scratch = refs[BIAS_PARTS:]
    weights = scratch[-1]
    even, odd = scratch[0:2], scratch[2:4]
    step = pl.program_id(0)
    yl, core, zl, x = (spot_ref[i] for i in range(4))
    head_rows = (iota((BLOCK, HEADS, WIDTH), 2) // HEAD_DIM) == iota((BLOCK, HEADS, WIDTH), 1)

    def rows_of(s):
        return pl.ds(pl.multiple_of(s * BLOCK, BLOCK), BLOCK)

    def score(buffers):
        scores, highest = buffers
        rows = rows_of(step)
        queries = (dot(own_ref[0, rows, :], wq_ref[...]) * (1.0 / math.sqrt(HEAD_DIM))).astype(BF16).astype(F32)
        spread = (
            jnp.where(head_rows, jnp.broadcast_to(queries[:, None, :], (BLOCK, HEADS, WIDTH)), 0.0)
            .reshape(QH, WIDTH)
            .astype(BF16)
        )
        top = jnp.full((8, QH), -3e38, F32)
        mask_rows = live[rows, : 2 * len(SPOTS)]
        for t in range(KEYS // KEY_TILE):
            blocks = [(b // 2, b % 2) for b in range(t * PER_TILE, (t + 1) * PER_TILE)]
            lanes = slice(t * KEY_TILE, (t + 1) * KEY_TILE)
            bias = []
            for i, slot in blocks:
                flip, back, side = SPOTS[i]
                block = (yl ^ slot) * 16 + (core ^ side) * 8 + (zl ^ flip) * 4 + (x + 4 - back) % 4
                bias += [part[block] for part in bias_refs]
            product = dot(key_ref[0, lanes, :], spread, NT) + jnp.concatenate(bias, axis=0).astype(F32)
            alive = jnp.concatenate([mask_rows[:, 2 * i + slot : 2 * i + slot + 1] for i, slot in blocks], axis=0)
            product = jnp.where(alive > 0.0, product, MASKED)
            scores[lanes, :] = product
            top = jnp.maximum(top, jnp.max(product.reshape(KEY_TILE // 8, 8, QH), axis=0))
            yield
        highest[...] = jnp.broadcast_to(jnp.max(top, axis=0, keepdims=True), (8, QH))

    def attend(buffers):
        scores, highest = buffers
        rows = rows_of(step - 1)
        largest = highest[0:1, :]
        total = jnp.zeros((8, QH), F32)
        for t in range(KEYS // KEY_TILE):
            lanes = slice(t * KEY_TILE, (t + 1) * KEY_TILE)
            expo = jnp.exp(scores[lanes, :] - largest)
            total = total + jnp.sum(expo.reshape(KEY_TILE // 8, 8, QH), axis=0)
            weights[lanes, :] = expo.astype(BF16)
            yield
        mixed = dot(value_ref[0], weights[...])
        mixed = mixed / jnp.sum(total, axis=0, keepdims=True)
        picked = jnp.where(head_rows, mixed.T.reshape(BLOCK, HEADS, WIDTH), 0.0)
        attended = jnp.sum(picked, axis=1)
        gate = jax.nn.sigmoid(dot(own_ref[0, rows, :], wg_ref[...]))
        added = dot((gate * attended).astype(BF16), wo_ref[...])
        out_ref[rows, :] = (x_ref[rows, :].astype(F32) + added).astype(BF16)

    def run(*work):
        for _ in itertools.zip_longest(*work):
            pass

    @pl.when(step == 0)
    def _():
        out_ref[SEQS * BLOCK :, :] = x_ref[SEQS * BLOCK :, :]
        run(score(even))

    @pl.when(step % 2 == 1)
    def _():
        run(score(odd), attend(even))

    @pl.when(step == 2)
    def _():
        run(score(even), attend(odd))

    @pl.when(step == SEQS)
    def _():
        run(attend(odd))


def row_attention(spot, own, x, keys, values, live, biases, wq, wg, wo):
    whole = lambda shape: pl.BlockSpec(shape, lambda s: (0,) * len(shape))
    square = whole((WIDTH, WIDTH))
    return pl.pallas_call(
        row_body,
        grid=(SEQS + 1,),
        in_specs=[
            pl.BlockSpec(memory_space=pltpu.SMEM),
            whole((2, CHUNK, WIDTH)),
            whole((CHUNK, WIDTH)),
            pl.BlockSpec((1, KEYS, WIDTH), lambda s: (jnp.minimum(s, SEQS - 1), 0, 0)),
            pl.BlockSpec((1, WIDTH, KEYS), lambda s: (jnp.maximum(s - 1, 0), 0, 0)),
            whole((WIDTH, 128)),
            *([whole((KEYS // BLOCK, BLOCK // BIAS_PARTS, QH))] * BIAS_PARTS),
            square,
            square,
            square,
        ],
        out_specs=whole((CHUNK, WIDTH)),
        out_shape=jax.ShapeDtypeStruct((CHUNK, WIDTH), BF16),
        scratch_shapes=[
            *([pltpu.VMEM((KEYS, QH), F32), pltpu.VMEM((8, QH), F32)] * 2),
            pltpu.VMEM((KEYS, QH), BF16),
        ],
        compiler_params=pltpu.CompilerParams(vmem_limit_bytes=57 << 20),
        cost_estimate=pl.CostEstimate(flops=12 << 30, bytes_accessed=12 << 20, transcendentals=4 << 20),
        name="row_attention",
    )(spot, own, x, keys, values, live, *biases, wq, wg, wo)


PART = 16
PART_ROWS = ALL_SEQS * PART
BACK = SEQS * BLOCK + 3 * BLOCK
SIDE = LEFT + 128


def column_body(
    mine_ref, x0_ref, x1_ref, x2_ref, x3_ref, w_ref, wo_ref, left_ref, right_ref, out_ref, a_ref, masks,
):
    x_refs = (x0_ref, x1_ref, x2_ref, x3_ref)
    mine = mine_ref[0]
    for b in range(4):
        lanes = x_refs[b][SEQS * BLOCK :, :].astype(F32)
        masks[:, b * 128 : b * 128 + 8] = lanes.T
    one_row = iota((PART_ROWS, PART_ROWS), 0)
    one_col = iota((PART_ROWS, PART_ROWS), 1)
    same = (one_row % PART) == (one_col % PART)

    def sequence(shape):
        slot = iota(shape, 0) // PART
        return ((slot // SEQS) ^ mine) * SEQS + slot % SEQS

    keep = iota((PART_ROWS, LEFT), 1) % ALL_SEQS == sequence((PART_ROWS, LEFT))
    keep_flag = iota((PART_ROWS, 128), 1) == sequence((PART_ROWS, 128))
    lane_head = iota((PART_ROWS, WIDTH), 1) // HEAD_DIM
    for g in range(BLOCK // PART):
        spots = [(s // SEQS, (s % SEQS) * BLOCK + g * PART) for s in range(ALL_SEQS)]
        data = jnp.concatenate([x_refs[b][r : r + PART, :] for b, r in spots], axis=0).astype(F32)
        filled = jnp.concatenate([masks[r : r + PART, b * 128 : b * 128 + 1] for b, r in spots], axis=0)
        live = jnp.concatenate([masks[r : r + PART, b * 128 + 1 : b * 128 + 2] for b, r in spots], axis=0)
        filled_lane = jnp.broadcast_to(filled, (PART_ROWS, 128)).T[0:1, :]
        fill = jnp.where(same, MASKED, OTHER)
        use = jnp.logical_and(same, jnp.broadcast_to(filled_lane, (PART_ROWS, PART_ROWS)) > 0.0)
        line = dot(norm(data).astype(BF16), w_ref[...])
        queries = (line[:, :WIDTH] * (1.0 / math.sqrt(HEAD_DIM))).astype(BF16)
        keys = line[:, WIDTH : 2 * WIDTH].astype(BF16)
        value = line[:, 2 * WIDTH : 3 * WIDTH].astype(BF16)
        gate = jax.nn.sigmoid(line[:, 3 * WIDTH :])
        mixed = jnp.zeros((PART_ROWS, WIDTH), F32)
        for h in range(HEADS):
            head = lane_head == h
            product = dot(jnp.where(head, queries, jnp.zeros_like(queries)), keys, NT)
            product = jnp.where(use, product, fill)
            expo = jnp.exp(product - jnp.max(product, axis=1, keepdims=True))
            total = jnp.sum(expo, axis=1, keepdims=True)
            mixed = mixed + jnp.where(head, dot(expo.astype(BF16), value) / total, 0.0)
        result = (data + dot((gate * mixed).astype(BF16), wo_ref[...])).astype(BF16)
        for s in range(SEQS):
            out_ref[s * BLOCK + g * PART : s * BLOCK + (g + 1) * PART, :] = result[s * PART : (s + 1) * PART]
        normed = norm(result.astype(F32)).astype(BF16)
        flags = jnp.where(keep_flag, jnp.broadcast_to(live, (PART_ROWS, 128)), 0.0)
        flags = jnp.sum(flags.reshape(ALL_SEQS, PART, 128), axis=0).astype(BF16)
        for weight_ref, out in ((right_ref, out_ref), (left_ref, a_ref)):
            wide = (dot(normed, weight_ref[...]) * live).astype(BF16).astype(F32)
            wide = jnp.where(keep, wide, 0.0)
            wide = jnp.sum(wide.reshape(ALL_SEQS, PART, LEFT), axis=0).astype(BF16)
            rows = slice(g * PART, (g + 1) * PART)
            if out is out_ref:
                first = SEQS * BLOCK + g * PART
                out[first : first + PART, :] = wide[:, :WIDTH]
                out[first + BLOCK : first + BLOCK + PART, :] = wide[:, WIDTH:]
                out[first + 2 * BLOCK : first + 2 * BLOCK + PART, :128] = flags
                out[first + 2 * BLOCK : first + 2 * BLOCK + PART, 128:] = flags
            else:
                for k in range(out.shape[0]):
                    out[k, rows, :LEFT] = wide
                    out[k, rows, LEFT:] = flags


def column_attention(mine, rows, query_matrix, final_matrix, side_matrix):
    left = jnp.repeat(side_matrix[:, :OUTER], ALL_SEQS, axis=1)
    right = jnp.repeat(side_matrix[:, OUTER:], ALL_SEQS, axis=1)
    vmem = pl.BlockSpec(memory_space=pltpu.VMEM)
    return pl.pallas_call(
        column_body,
        in_specs=[pl.BlockSpec(memory_space=pltpu.SMEM)] + [vmem] * 8,
        out_specs=[vmem] * 2,
        out_shape=[
            jax.ShapeDtypeStruct((BACK, WIDTH), BF16),
            jax.ShapeDtypeStruct((8, BLOCK, SIDE), BF16),
        ],
        scratch_shapes=[pltpu.VMEM((WIDTH, 512), F32)],
        compiler_params=pltpu.CompilerParams(vmem_limit_bytes=24 << 20),
        cost_estimate=pl.CostEstimate(flops=4 << 30, bytes_accessed=3 << 20, transcendentals=2 << 20),
        name="column_attention",
    )(mine, *rows, query_matrix, final_matrix, left, right)


PAIR_STEP = 128
WIDE = BLOCK * PAIR
STRIDE = BLOCK + 8


def pair_body(a_ref, b_ref, w_ref, pair_ref, out_ref, table, update):
    @pl.when(pl.program_id(0) == 0)
    def _():
        keep = (iota((16 * ALL_SEQS, LEFT), 1) % ALL_SEQS) == (iota((16 * ALL_SEQS, LEFT), 0) % ALL_SEQS)
        fold = (iota((LEFT, 128), 0) // ALL_SEQS == iota((LEFT, 128), 1)).astype(BF16)

        def build(q, carry):
            first = pl.multiple_of(SEQS * BLOCK + q * 16, 16)
            rows = jnp.concatenate(
                [b_ref[pl.ds(first, 16), :], b_ref[pl.ds(pl.multiple_of(first + BLOCK, 16), 16), :]], axis=1
            ).astype(F32)
            rows = jnp.broadcast_to(rows[:, None, :], (16, ALL_SEQS, LEFT)).reshape(16 * ALL_SEQS, LEFT)
            right = dot(jnp.where(keep, rows, 0.0).astype(BF16), fold).astype(BF16)
            for c in range(OUTER // 2):
                part = dot(right, w_ref[:, c * 256 : (c + 1) * 256]).astype(BF16)
                for j in range(16):
                    lanes = pl.ds(pl.multiple_of((q * 16 + j) * PAIR, PAIR), PAIR)
                    for d in range(2):
                        table[(2 * c + d) * 16 : (2 * c + d + 1) * 16, lanes] = part[
                            j * 16 : (j + 1) * 16, d * PAIR : (d + 1) * PAIR
                        ]
            return carry

        lax.fori_loop(0, BLOCK // 16, build, 0)

    left = a_ref[:, :LEFT]
    count = dot(a_ref[:, LEFT:], b_ref[BACK - BLOCK :, :128], NT)
    scale = 1.0 / jnp.maximum(count, 1.0)
    per_dot = 4
    for j in range(0, BLOCK, per_dot):
        part = dot(left, table[:, j * PAIR : (j + per_dot) * PAIR])
        for d in range(per_dot):
            update[pl.ds(j + d, PAIR_STEP, stride=STRIDE), :] = (
                part[:, d * PAIR : (d + 1) * PAIR] * scale[:, j + d : j + d + 1]
            )

    def finish(i, carry):
        rows = update[pl.ds(pl.multiple_of(i * STRIDE, 8), BLOCK), :]
        out_ref[i] = (pair_ref[i].astype(F32) + rows).astype(BF16)
        return carry

    lax.fori_loop(0, PAIR_STEP, finish, 0, unroll=4)


def pair_update(left, right, final_matrix, couple_state):
    wide = final_matrix.reshape(OUTER, OUTER, PAIR).transpose(1, 0, 2).reshape(OUTER, OUTER * PAIR)
    wide = jnp.pad(wide, ((0, 128 - OUTER), (0, 0)))
    block = pl.BlockSpec((PAIR_STEP, BLOCK, PAIR), lambda i: (i, 0, 0))
    return pl.pallas_call(
        pair_body,
        grid=(ROWS // PAIR_STEP,),
        in_specs=[
            pl.BlockSpec((PAIR_STEP, SIDE), lambda i: (i, 0)),
            pl.BlockSpec((BACK, WIDTH), lambda i: (0, 0)),
            pl.BlockSpec((128, OUTER * PAIR), lambda i: (0, 0)),
            block,
        ],
        out_specs=block,
        out_shape=jax.ShapeDtypeStruct(couple_state.shape, BF16),
        scratch_shapes=[
            pltpu.VMEM((LEFT, WIDE), BF16),
            pltpu.VMEM((STRIDE * PAIR_STEP, PAIR), F32),
        ],
        compiler_params=pltpu.CompilerParams(vmem_limit_bytes=53 << 20),
        cost_estimate=pl.CostEstimate(flops=8 << 30, bytes_accessed=18 << 20, transcendentals=0),
        name="pair_update",
    )(left, right, wide, couple_state)


def per_device(
    lineup_state,
    couple_state,
    lineup_filled,
    observed_amino_flag,
    horizontal_query_matrix,
    horizontal_final_matrix,
    couple_offset_matrix,
    vertical_query_matrix,
    vertical_final_matrix,
    tensor_mean_side_matrix,
    tensor_mean_final_matrix,
):
    spot = jnp.stack([lax.axis_index(axis) for axis in ("yl", "co", "zl", "x")]).astype(jnp.int32)
    block = lax.axis_index(RES).astype(jnp.int32).reshape(1)
    mine = (lax.axis_index("yh") * 2 + lax.axis_index("zh")).astype(jnp.int32).reshape(1)
    packed = pack_chunk(block, lineup_state, lineup_filled, observed_amino_flag)
    chunk = swap(packed)
    send = bias_blocks(couple_state, couple_offset_matrix, 0, 1)
    kept = norm_chunks(chunk, swap(packed, 1), send)
    parts = []
    for flip in (0, 1):
        part = shift(kept, 0, 1) if flip else kept
        parts += [part, shift(kept, 1, flip), shift(kept, -1, flip)]
    send = bias_blocks(couple_state, couple_offset_matrix, 1, 2, send, kept)
    send = bias_blocks(couple_state, couple_offset_matrix, 3, 1, send, *parts[1:])
    parts = parts[:3] + [shift(parts[1], 1)] + parts[3:] + [shift(parts[5], -1)]
    send = tie(send, parts[3], parts[7])
    parts += [lax.ppermute(part, "co", FLIP) for part in parts]
    biases = [lax.all_to_all(send.reshape((32,) + send.shape[2:]), RES, 0, 0)]
    wq, wk, wv, wg = (horizontal_query_matrix[:, i * WIDTH : (i + 1) * WIDTH] for i in range(4))
    keys, values, live = row_keys(parts, wk, wv)
    rows = row_attention(spot, kept, chunk, keys, values, live, biases, wq, wg, horizontal_final_matrix)
    rows = [rows] + [lax.ppermute(rows, COLUMN, [(i, i ^ k) for i in range(4)]) for k in (1, 2, 3)]
    back, left = column_attention(
        mine, rows, vertical_query_matrix, vertical_final_matrix, tensor_mean_side_matrix
    )
    back = swap(back)
    left = lax.all_to_all(left, NEAR, 0, 0)
    pair = pair_update(left.reshape(ROWS, SIDE), back, tensor_mean_final_matrix, couple_state)
    return back[: SEQS * BLOCK].reshape(SEQS, BLOCK, WIDTH), pair


def solution(mesh):
    fine = Mesh(mesh.devices.reshape(SIZES), AXES)
    return jax.shard_map(
        per_device,
        mesh=fine,
        in_specs=(
            P(SEQ, RES, None),
            P(SEQ, RES, None),
            P(SEQ, RES),
            P(),
            P(),
            P(),
            P(),
            P(),
            P(),
            P(),
            P(),
        ),
        out_specs=(P(SEQ, RES, None), P(SEQ, RES, None)),
        check_vma=False,
    )
```

```python
import itertools
import math

import jax
import jax.numpy as jnp
import numpy as np
from jax import lax
from jax.experimental import pallas as pl
from jax.experimental.pallas import tpu as pltpu
from jax.sharding import Mesh, PartitionSpec as P

F32 = jnp.float32
BF16 = jnp.bfloat16

AXES = ("yl", "co", "yh", "zh", "zl", "x")
SIZES = (2, 2, 2, 2, 2, 4)
SEQ = ("yl", "co")
RES = ("yh", "zh", "zl", "x")
SWAPPED = ("yl", "co", "yh", "zh")
COLUMN = ("yh", "zh")
NEAR = ("zl", "x")

SEQS = 4
BLOCK = 64
ROWS = 512
WIDTH = 256
HEADS = 8
HEAD_DIM = 32
ALL_SEQS = 16
OUTER = 32
PAIR = 128
LEFT = ALL_SEQS * OUTER
CHUNK = SEQS * BLOCK + 8
MASKED = -1000000000.0
OTHER = -2000000000.0

FLIP = [(0, 1), (1, 0)]
NT = (((1,), (1,)), ((), ()))


def swap_pairs(flip):
    pairs = []
    for spot in np.ndindex(2, 2, 2, 2):
        target = (spot[2] ^ flip, spot[3], spot[0], spot[1])
        pairs.append(
            (int(np.ravel_multi_index(spot, (2, 2, 2, 2))), int(np.ravel_multi_index(target, (2, 2, 2, 2))))
        )
    return pairs


def swap(array, flip=0):
    return lax.ppermute(array, SWAPPED, swap_pairs(flip))


def shift(array, step, flip=0):
    return lax.ppermute(array, NEAR, [(z * 4 + i, (z ^ flip) * 4 + (i + step) % 4) for z in (0, 1) for i in range(4)])


def tie_body(*refs):
    pass


def tie(array, *first):
    anywhere = pl.BlockSpec(memory_space=pl.ANY)
    return pl.pallas_call(
        tie_body,
        in_specs=[anywhere] * (1 + len(first)),
        out_specs=anywhere,
        out_shape=jax.ShapeDtypeStruct(array.shape, array.dtype),
        input_output_aliases={0: 0},
        name="tie",
    )(array, *first)


def dot(a, b, dims=(((1,), (0,)), ((), ()))):
    return lax.dot_general(a, b, dims, preferred_element_type=F32)


def norm(data):
    centered = data - jnp.mean(data, axis=-1, keepdims=True)
    variance = jnp.mean(centered * centered, axis=-1, keepdims=True)
    return centered * lax.rsqrt(variance + 1e-05)


def iota(shape, dim):
    return lax.broadcasted_iota(jnp.int32, shape, dim)


def pack_body(block_ref, x_ref, filled_ref, flag_ref, out_ref):
    rows = SEQS * BLOCK
    out_ref[:rows, :] = x_ref[...]
    filled = filled_ref[...].astype(F32)
    block = block_ref[0]
    flags = flag_ref[pl.ds(block // 2, 1), :].astype(F32)
    live = filled * jnp.where(block % 2 == 0, flags[:, :BLOCK], flags[:, BLOCK:])
    lines = [jnp.concatenate([part[i : i + 1] for i in range(SEQS)], axis=1) for part in (filled, live)]
    lines.append(jnp.zeros((6, WIDTH), F32))
    out_ref[rows:, :] = jnp.concatenate(lines, axis=0).astype(BF16)


def pack_chunk(block, lineup_state, lineup_filled, flags):
    vmem = pl.BlockSpec(memory_space=pltpu.VMEM)
    return pl.pallas_call(
        pack_body,
        in_specs=[pl.BlockSpec(memory_space=pltpu.SMEM), vmem, vmem, vmem],
        out_specs=vmem,
        out_shape=jax.ShapeDtypeStruct((CHUNK, WIDTH), BF16),
        name="pack_lineup",
    )(block, lineup_state.reshape(SEQS * BLOCK, WIDTH), lineup_filled, flags.reshape(-1, 2 * BLOCK))


def norm_body(x_ref, flipped_ref, after_ref, out_ref):
    rows = SEQS * BLOCK
    for slot, ref in enumerate((x_ref, flipped_ref)):
        out_ref[slot, :rows, :] = norm(ref[:rows, :].astype(F32)).astype(BF16)
        out_ref[slot, rows:, :] = ref[rows:, :]


def norm_chunks(chunk, flipped, after):
    vmem = pl.BlockSpec(memory_space=pltpu.VMEM)
    return pl.pallas_call(
        norm_body,
        in_specs=[vmem, vmem, pl.BlockSpec(memory_space=pl.ANY)],
        out_shape=jax.ShapeDtypeStruct((2, CHUNK, WIDTH), BF16),
        name="norm_lineup",
    )(chunk, flipped, after)


BIAS_STEP = 128
BIAS_PARTS = 1
GROUP = 32
COPIES = 4


def bias_body(pair_ref, weight_ref, *refs):
    out_ref, spread, normed = refs[-3:]

    @pl.when(pl.program_id(0) == 0)
    def _():
        wide = weight_ref[...]
        owner = iota((PAIR, WIDTH), 1) // HEADS

        def place(i, carry):
            spread[pl.ds(pl.multiple_of(i * PAIR, PAIR), PAIR), :] = jnp.where(
                owner == i, wide, jnp.zeros_like(wide)
            )
            return carry

        lax.fori_loop(0, GROUP, place, 0)

    groups = BIAS_STEP // GROUP
    cols = BLOCK // BIAS_PARTS
    ones = jnp.ones((PAIR, PAIR), BF16)

    def one(i, carry):
        for g in range(groups):
            raw = pair_ref[g * GROUP + i]
            centered = raw.astype(F32) - dot(raw, ones) * (1.0 / PAIR)
            variance = jnp.mean(centered * centered, axis=-1, keepdims=True)
            normed[g * cols : (g + 1) * cols, pl.ds(pl.multiple_of(i * PAIR, PAIR), PAIR)] = (
                centered * lax.rsqrt(variance + 1e-05)
            ).astype(BF16)
        return carry

    lax.fori_loop(0, GROUP, one, 0, unroll=8)
    result = dot(normed[...], spread[...]).astype(BF16)
    for g in range(groups):
        for c in range(COPIES):
            out_ref[c, g // 2, :, (g % 2) * WIDTH : (g % 2 + 1) * WIDTH] = result[g * cols : (g + 1) * cols]


def bias_blocks(couple_state, couple_offset_matrix, start, steps, *after):
    wide = jnp.tile(couple_offset_matrix, (1, GROUP))
    per_step = BIAS_STEP // BLOCK
    cols = BLOCK // BIAS_PARTS
    return pl.pallas_call(
        bias_body,
        grid=(steps,),
        in_specs=[
            pl.BlockSpec((BIAS_STEP, cols, PAIR), lambda i: (i + start, 0, 0)),
            pl.BlockSpec((PAIR, WIDTH), lambda i: (0, 0)),
        ]
        + [pl.BlockSpec(memory_space=pl.ANY)] * len(after),
        out_specs=pl.BlockSpec((COPIES, per_step, cols, BLOCK * HEADS), lambda i: (0, i + start, 0, 0)),
        out_shape=jax.ShapeDtypeStruct((COPIES, ROWS // BLOCK, cols, BLOCK * HEADS), BF16),
        scratch_shapes=[
            pltpu.VMEM((GROUP * PAIR, WIDTH), BF16),
            pltpu.VMEM((BIAS_STEP // GROUP * cols, GROUP * PAIR), BF16),
        ],
        compiler_params=pltpu.CompilerParams(vmem_limit_bytes=53 << 20),
        cost_estimate=pl.CostEstimate(flops=8 << 30, bytes_accessed=6 << 20, transcendentals=0),
        input_output_aliases={2: 0} if start else {},
        name="pair_bias",
    )(couple_state, wide, *after)


KEY_TILE = 512
KEYS = 2048
QH = BLOCK * HEADS
PER_TILE = KEY_TILE // BLOCK
SPOTS = [(zl, x, co) for co in (0, 1) for zl in (0, 1) for x in (0, 1, 3, 2)]


def key_body(*refs):
    parts, flags = refs[: len(SPOTS)], refs[len(SPOTS) : 2 * len(SPOTS)]
    wk_ref, wvt_ref, key_ref, value_ref, live_ref = refs[2 * len(SPOTS) :]

    @pl.when(pl.program_id(0) == 0)
    def _():
        lanes = jnp.concatenate([ref[...].astype(F32)[:, 1, :] for ref in flags], axis=0)
        live_ref[...] = jnp.concatenate([lanes, jnp.zeros((128 - 2 * len(SPOTS), WIDTH), F32)], axis=0).T

    for t in range(KEYS // KEY_TILE):
        blocks = [(b // 2, b % 2) for b in range(t * PER_TILE, (t + 1) * PER_TILE)]
        tile = jnp.concatenate([parts[i][slot] for i, slot in blocks], axis=0)
        lanes = slice(t * KEY_TILE, (t + 1) * KEY_TILE)
        key_ref[0, lanes, :] = dot(tile, wk_ref[...]).astype(BF16)
        value_ref[0, :, lanes] = dot(wvt_ref[...], tile, NT).astype(BF16)


def row_keys(parts, wk, wv):
    gathered = pl.BlockSpec((2, BLOCK, WIDTH), lambda s: (0, s, 0))
    masks = pl.BlockSpec((2, 8, WIDTH), lambda s: (0, SEQS * BLOCK // 8, 0))
    square = pl.BlockSpec((WIDTH, WIDTH), lambda s: (0, 0))
    return pl.pallas_call(
        key_body,
        grid=(SEQS,),
        in_specs=[*([gathered] * len(SPOTS)), *([masks] * len(SPOTS)), square, square],
        out_specs=[
            pl.BlockSpec((1, KEYS, WIDTH), lambda s: (s, 0, 0)),
            pl.BlockSpec((1, WIDTH, KEYS), lambda s: (s, 0, 0)),
            pl.BlockSpec((WIDTH, 128), lambda s: (0, 0)),
        ],
        out_shape=[
            jax.ShapeDtypeStruct((SEQS, KEYS, WIDTH), BF16),
            jax.ShapeDtypeStruct((SEQS, WIDTH, KEYS), BF16),
            jax.ShapeDtypeStruct((WIDTH, 128), F32),
        ],
        compiler_params=pltpu.CompilerParams(vmem_limit_bytes=57 << 20),
        cost_estimate=pl.CostEstimate(flops=4 << 30, bytes_accessed=12 << 20, transcendentals=0),
        name="row_keys",
    )(*parts, *parts, wk, wv.T)


def row_body(spot_ref, own_ref, x_ref, key_ref, value_ref, live, *refs):
    bias_refs = refs[:BIAS_PARTS]
    wq_ref, wg_ref, wo_ref, out_ref, *scratch = refs[BIAS_PARTS:]
    weights = scratch[-1]
    even, odd = scratch[0:2], scratch[2:4]
    step = pl.program_id(0)
    yl, core, zl, x = (spot_ref[i] for i in range(4))
    head_rows = (iota((BLOCK, HEADS, WIDTH), 2) // HEAD_DIM) == iota((BLOCK, HEADS, WIDTH), 1)

    def rows_of(s):
        return pl.ds(pl.multiple_of(s * BLOCK, BLOCK), BLOCK)

    def score(buffers):
        scores, highest = buffers
        rows = rows_of(step)
        queries = (dot(own_ref[0, rows, :], wq_ref[...]) * (1.0 / math.sqrt(HEAD_DIM))).astype(BF16).astype(F32)
        spread = (
            jnp.where(head_rows, jnp.broadcast_to(queries[:, None, :], (BLOCK, HEADS, WIDTH)), 0.0)
            .reshape(QH, WIDTH)
            .astype(BF16)
        )
        top = jnp.full((8, QH), -3e38, F32)
        mask_rows = live[rows, : 2 * len(SPOTS)]
        for t in range(KEYS // KEY_TILE):
            blocks = [(b // 2, b % 2) for b in range(t * PER_TILE, (t + 1) * PER_TILE)]
            lanes = slice(t * KEY_TILE, (t + 1) * KEY_TILE)
            bias = []
            for i, slot in blocks:
                flip, back, side = SPOTS[i]
                block = (yl ^ slot) * 16 + (core ^ side) * 8 + (zl ^ flip) * 4 + (x + 4 - back) % 4
                bias += [part[block] for part in bias_refs]
            product = dot(key_ref[0, lanes, :], spread, NT) + jnp.concatenate(bias, axis=0).astype(F32)
            alive = jnp.concatenate([mask_rows[:, 2 * i + slot : 2 * i + slot + 1] for i, slot in blocks], axis=0)
            product = jnp.where(alive > 0.0, product, MASKED)
            scores[lanes, :] = product
            top = jnp.maximum(top, jnp.max(product.reshape(KEY_TILE // 8, 8, QH), axis=0))
            yield
        highest[...] = jnp.broadcast_to(jnp.max(top, axis=0, keepdims=True), (8, QH))

    def attend(buffers):
        scores, highest = buffers
        rows = rows_of(step - 1)
        largest = highest[0:1, :]
        total = jnp.zeros((8, QH), F32)
        for t in range(KEYS // KEY_TILE):
            lanes = slice(t * KEY_TILE, (t + 1) * KEY_TILE)
            expo = jnp.exp(scores[lanes, :] - largest)
            total = total + jnp.sum(expo.reshape(KEY_TILE // 8, 8, QH), axis=0)
            weights[lanes, :] = expo.astype(BF16)
            yield
        mixed = dot(value_ref[0], weights[...])
        mixed = mixed / jnp.sum(total, axis=0, keepdims=True)
        picked = jnp.where(head_rows, mixed.T.reshape(BLOCK, HEADS, WIDTH), 0.0)
        attended = jnp.sum(picked, axis=1)
        gate = jax.nn.sigmoid(dot(own_ref[0, rows, :], wg_ref[...]))
        added = dot((gate * attended).astype(BF16), wo_ref[...])
        out_ref[rows, :] = (x_ref[rows, :].astype(F32) + added).astype(BF16)

    def run(*work):
        for _ in itertools.zip_longest(*work):
            pass

    @pl.when(step == 0)
    def _():
        out_ref[SEQS * BLOCK :, :] = x_ref[SEQS * BLOCK :, :]
        run(score(even))

    @pl.when(step % 2 == 1)
    def _():
        run(score(odd), attend(even))

    @pl.when(step == 2)
    def _():
        run(score(even), attend(odd))

    @pl.when(step == SEQS)
    def _():
        run(attend(odd))


def row_attention(spot, own, x, keys, values, live, biases, wq, wg, wo):
    whole = lambda shape: pl.BlockSpec(shape, lambda s: (0,) * len(shape))
    square = whole((WIDTH, WIDTH))
    return pl.pallas_call(
        row_body,
        grid=(SEQS + 1,),
        in_specs=[
            pl.BlockSpec(memory_space=pltpu.SMEM),
            whole((2, CHUNK, WIDTH)),
            whole((CHUNK, WIDTH)),
            pl.BlockSpec((1, KEYS, WIDTH), lambda s: (jnp.minimum(s, SEQS - 1), 0, 0)),
            pl.BlockSpec((1, WIDTH, KEYS), lambda s: (jnp.maximum(s - 1, 0), 0, 0)),
            whole((WIDTH, 128)),
            *([whole((KEYS // BLOCK, BLOCK // BIAS_PARTS, QH))] * BIAS_PARTS),
            square,
            square,
            square,
        ],
        out_specs=whole((CHUNK, WIDTH)),
        out_shape=jax.ShapeDtypeStruct((CHUNK, WIDTH), BF16),
        scratch_shapes=[
            *([pltpu.VMEM((KEYS, QH), F32), pltpu.VMEM((8, QH), F32)] * 2),
            pltpu.VMEM((KEYS, QH), BF16),
        ],
        compiler_params=pltpu.CompilerParams(vmem_limit_bytes=57 << 20),
        cost_estimate=pl.CostEstimate(flops=12 << 30, bytes_accessed=12 << 20, transcendentals=4 << 20),
        name="row_attention",
    )(spot, own, x, keys, values, live, *biases, wq, wg, wo)


PART = 16
PART_ROWS = ALL_SEQS * PART
BACK = SEQS * BLOCK + 3 * BLOCK
SIDE = LEFT + 128


def column_body(
    mine_ref, x0_ref, x3_ref, x2_ref, x1_ref, w_ref, wo_ref, left_ref, right_ref, out_ref, a_ref, masks,
):
    x_refs = (x0_ref, x1_ref, x2_ref, x3_ref)
    mine = mine_ref[0]
    for b in range(4):
        lanes = x_refs[b][SEQS * BLOCK :, :].astype(F32)
        masks[:, b * 128 : b * 128 + 8] = lanes.T
    one_row = iota((PART_ROWS, PART_ROWS), 0)
    one_col = iota((PART_ROWS, PART_ROWS), 1)
    same = (one_row % PART) == (one_col % PART)

    def sequence(shape):
        slot = iota(shape, 0) // PART
        return ((slot // SEQS) ^ mine) * SEQS + slot % SEQS

    keep = iota((PART_ROWS, LEFT), 1) % ALL_SEQS == sequence((PART_ROWS, LEFT))
    keep_flag = iota((PART_ROWS, 128), 1) == sequence((PART_ROWS, 128))
    lane_head = iota((PART_ROWS, WIDTH), 1) // HEAD_DIM
    for g in range(BLOCK // PART):
        spots = [(s // SEQS, (s % SEQS) * BLOCK + g * PART) for s in range(ALL_SEQS)]
        data = jnp.concatenate([x_refs[b][r : r + PART, :] for b, r in spots], axis=0).astype(F32)
        filled = jnp.concatenate([masks[r : r + PART, b * 128 : b * 128 + 1] for b, r in spots], axis=0)
        live = jnp.concatenate([masks[r : r + PART, b * 128 + 1 : b * 128 + 2] for b, r in spots], axis=0)
        filled_lane = jnp.broadcast_to(filled, (PART_ROWS, 128)).T[0:1, :]
        fill = jnp.where(same, MASKED, OTHER)
        use = jnp.logical_and(same, jnp.broadcast_to(filled_lane, (PART_ROWS, PART_ROWS)) > 0.0)
        line = dot(norm(data).astype(BF16), w_ref[...])
        queries = (line[:, :WIDTH] * (1.0 / math.sqrt(HEAD_DIM))).astype(BF16)
        keys = line[:, WIDTH : 2 * WIDTH].astype(BF16)
        value = line[:, 2 * WIDTH : 3 * WIDTH].astype(BF16)
        gate = jax.nn.sigmoid(line[:, 3 * WIDTH :])
        mixed = jnp.zeros((PART_ROWS, WIDTH), F32)
        for h in range(HEADS):
            head = lane_head == h
            product = dot(jnp.where(head, queries, jnp.zeros_like(queries)), keys, NT)
            product = jnp.where(use, product, fill)
            expo = jnp.exp(product - jnp.max(product, axis=1, keepdims=True))
            total = jnp.sum(expo, axis=1, keepdims=True)
            mixed = mixed + jnp.where(head, dot(expo.astype(BF16), value) / total, 0.0)
        result = (data + dot((gate * mixed).astype(BF16), wo_ref[...])).astype(BF16)
        for s in range(SEQS):
            out_ref[s * BLOCK + g * PART : s * BLOCK + (g + 1) * PART, :] = result[s * PART : (s + 1) * PART]
        normed = norm(result.astype(F32)).astype(BF16)
        flags = jnp.where(keep_flag, jnp.broadcast_to(live, (PART_ROWS, 128)), 0.0)
        flags = jnp.sum(flags.reshape(ALL_SEQS, PART, 128), axis=0).astype(BF16)
        for weight_ref, out in ((right_ref, out_ref), (left_ref, a_ref)):
            wide = (dot(normed, weight_ref[...]) * live).astype(BF16).astype(F32)
            wide = jnp.where(keep, wide, 0.0)
            wide = jnp.sum(wide.reshape(ALL_SEQS, PART, LEFT), axis=0).astype(BF16)
            rows = slice(g * PART, (g + 1) * PART)
            if out is out_ref:
                first = SEQS * BLOCK + g * PART
                out[first : first + PART, :] = wide[:, :WIDTH]
                out[first + BLOCK : first + BLOCK + PART, :] = wide[:, WIDTH:]
                out[first + 2 * BLOCK : first + 2 * BLOCK + PART, :128] = flags
                out[first + 2 * BLOCK : first + 2 * BLOCK + PART, 128:] = flags
            else:
                for k in range(out.shape[0]):
                    out[k, rows, :LEFT] = wide
                    out[k, rows, LEFT:] = flags


def column_attention(mine, rows, query_matrix, final_matrix, side_matrix):
    left = jnp.repeat(side_matrix[:, :OUTER], ALL_SEQS, axis=1)
    right = jnp.repeat(side_matrix[:, OUTER:], ALL_SEQS, axis=1)
    vmem = pl.BlockSpec(memory_space=pltpu.VMEM)
    return pl.pallas_call(
        column_body,
        in_specs=[pl.BlockSpec(memory_space=pltpu.SMEM)] + [vmem] * 8,
        out_specs=[vmem] * 2,
        out_shape=[
            jax.ShapeDtypeStruct((BACK, WIDTH), BF16),
            jax.ShapeDtypeStruct((8, BLOCK, SIDE), BF16),
        ],
        scratch_shapes=[pltpu.VMEM((WIDTH, 512), F32)],
        compiler_params=pltpu.CompilerParams(vmem_limit_bytes=24 << 20),
        cost_estimate=pl.CostEstimate(flops=4 << 30, bytes_accessed=3 << 20, transcendentals=2 << 20),
        name="column_attention",
    )(mine, *rows, query_matrix, final_matrix, left, right)


PAIR_STEP = 128
WIDE = BLOCK * PAIR
STRIDE = BLOCK + 8


def pair_body(a_ref, b_ref, w_ref, pair_ref, out_ref, aligned_ref, table, even, odd):
    step = pl.program_id(0)
    steps = ROWS // PAIR_STEP
    per_dot = 4

    def multiply(update):
        left = a_ref[:, :LEFT]
        count = dot(a_ref[:, LEFT:], b_ref[BACK - BLOCK :, :128], NT)
        scale = 1.0 / jnp.maximum(count, 1.0)
        for j in range(0, BLOCK, per_dot):
            part = dot(left, table[:, j * PAIR : (j + per_dot) * PAIR])
            for d in range(per_dot):
                update[pl.ds(j + d, PAIR_STEP, stride=STRIDE), :] = (
                    part[:, d * PAIR : (d + 1) * PAIR] * scale[:, j + d : j + d + 1]
                )
            yield

    def finish(update):
        share = PAIR_STEP * per_dot // BLOCK
        for first in range(0, PAIR_STEP, share):
            for i in range(first, first + share):
                rows = update[i * STRIDE : i * STRIDE + BLOCK, :]
                out_ref[i] = (pair_ref[i].astype(F32) + rows).astype(BF16)
            yield

    def run(*work):
        for _ in itertools.zip_longest(*work):
            pass

    @pl.when(step == 0)
    def _():
        aligned_ref[...] = b_ref[: SEQS * BLOCK, :]
        keep = (iota((16 * ALL_SEQS, LEFT), 1) % ALL_SEQS) == (iota((16 * ALL_SEQS, LEFT), 0) % ALL_SEQS)
        fold = (iota((LEFT, 128), 0) // ALL_SEQS == iota((LEFT, 128), 1)).astype(BF16)

        def build(q, carry):
            first = pl.multiple_of(SEQS * BLOCK + q * 16, 16)
            rows = jnp.concatenate(
                [b_ref[pl.ds(first, 16), :], b_ref[pl.ds(pl.multiple_of(first + BLOCK, 16), 16), :]], axis=1
            ).astype(F32)
            rows = jnp.broadcast_to(rows[:, None, :], (16, ALL_SEQS, LEFT)).reshape(16 * ALL_SEQS, LEFT)
            right = dot(jnp.where(keep, rows, 0.0).astype(BF16), fold).astype(BF16)
            for c in range(OUTER // 2):
                part = dot(right, w_ref[:, c * 256 : (c + 1) * 256]).astype(BF16)
                for j in range(16):
                    lanes = pl.ds(pl.multiple_of((q * 16 + j) * PAIR, PAIR), PAIR)
                    for d in range(2):
                        table[(2 * c + d) * 16 : (2 * c + d + 1) * 16, lanes] = part[
                            j * 16 : (j + 1) * 16, d * PAIR : (d + 1) * PAIR
                        ]
            return carry

        lax.fori_loop(0, BLOCK // 16, build, 0)
        run(multiply(even))

    @pl.when(step % 2 == 1)
    def _():
        run(multiply(odd), finish(even))

    @pl.when(jnp.logical_and(step > 0, jnp.logical_and(step % 2 == 0, step < steps)))
    def _():
        run(multiply(even), finish(odd))

    @pl.when(step == steps)
    def _():
        run(finish(odd))


def pair_update(left, right, final_matrix, couple_state):
    wide = final_matrix.reshape(OUTER, OUTER, PAIR).transpose(1, 0, 2).reshape(OUTER, OUTER * PAIR)
    wide = jnp.pad(wide, ((0, 128 - OUTER), (0, 0)))
    steps = ROWS // PAIR_STEP
    block = pl.BlockSpec((PAIR_STEP, BLOCK, PAIR), lambda i: (jnp.maximum(i - 1, 0), 0, 0))
    return pl.pallas_call(
        pair_body,
        grid=(steps + 1,),
        in_specs=[
            pl.BlockSpec((PAIR_STEP, SIDE), lambda i: (jnp.minimum(i, steps - 1), 0)),
            pl.BlockSpec((BACK, WIDTH), lambda i: (0, 0)),
            pl.BlockSpec((128, OUTER * PAIR), lambda i: (0, 0)),
            block,
        ],
        out_specs=[block, pl.BlockSpec((SEQS * BLOCK, WIDTH), lambda i: (0, 0))],
        out_shape=[
            jax.ShapeDtypeStruct(couple_state.shape, BF16),
            jax.ShapeDtypeStruct((SEQS * BLOCK, WIDTH), BF16),
        ],
        scratch_shapes=[
            pltpu.VMEM((LEFT, WIDE), BF16),
            pltpu.VMEM((STRIDE * PAIR_STEP, PAIR), F32),
            pltpu.VMEM((STRIDE * PAIR_STEP, PAIR), F32),
        ],
        compiler_params=pltpu.CompilerParams(vmem_limit_bytes=57 << 20),
        cost_estimate=pl.CostEstimate(flops=8 << 30, bytes_accessed=18 << 20, transcendentals=0),
        name="pair_update",
    )(left, right, wide, couple_state)


def per_device(
    lineup_state,
    couple_state,
    lineup_filled,
    observed_amino_flag,
    horizontal_query_matrix,
    horizontal_final_matrix,
    couple_offset_matrix,
    vertical_query_matrix,
    vertical_final_matrix,
    tensor_mean_side_matrix,
    tensor_mean_final_matrix,
):
    spot = jnp.stack([lax.axis_index(axis) for axis in ("yl", "co", "zl", "x")]).astype(jnp.int32)
    block = lax.axis_index(RES).astype(jnp.int32).reshape(1)
    mine = (lax.axis_index("yh") * 2 + lax.axis_index("zh")).astype(jnp.int32).reshape(1)
    packed = pack_chunk(block, lineup_state, lineup_filled, observed_amino_flag)
    chunk = swap(packed)
    send = bias_blocks(couple_state, couple_offset_matrix, 0, 1)
    kept = norm_chunks(chunk, swap(packed, 1), send)
    parts = []
    for flip in (0, 1):
        part = shift(kept, 0, 1) if flip else kept
        parts += [part, shift(kept, 1, flip), shift(kept, -1, flip)]
    send = bias_blocks(couple_state, couple_offset_matrix, 1, 2, send, kept)
    send = bias_blocks(couple_state, couple_offset_matrix, 3, 1, send, *parts[1:])
    parts = parts[:3] + [shift(parts[1], 1)] + parts[3:] + [shift(parts[5], -1)]
    send = tie(send, parts[3], parts[7])
    parts += [lax.ppermute(part, "co", FLIP) for part in parts]
    biases = [lax.all_to_all(send.reshape((32,) + send.shape[2:]), RES, 0, 0)]
    wq, wk, wv, wg = (horizontal_query_matrix[:, i * WIDTH : (i + 1) * WIDTH] for i in range(4))
    keys, values, live = row_keys(parts, wk, wv)
    rows = row_attention(spot, kept, chunk, keys, values, live, biases, wq, wg, horizontal_final_matrix)
    rows = [rows] + [lax.ppermute(rows, COLUMN, [(i, i ^ k) for i in range(4)]) for k in (3, 2, 1)]
    back, left = column_attention(
        mine, rows, vertical_query_matrix, vertical_final_matrix, tensor_mean_side_matrix
    )
    back = swap(back)
    left = lax.all_to_all(left, NEAR, 0, 0)
    pair, aligned = pair_update(left.reshape(ROWS, SIDE), back, tensor_mean_final_matrix, couple_state)
    return aligned.reshape(SEQS, BLOCK, WIDTH), pair


def solution(mesh):
    fine = Mesh(mesh.devices.reshape(SIZES), AXES)
    return jax.shard_map(
        per_device,
        mesh=fine,
        in_specs=(
            P(SEQ, RES, None),
            P(SEQ, RES, None),
            P(SEQ, RES),
            P(),
            P(),
            P(),
            P(),
            P(),
            P(),
            P(),
            P(),
        ),
        out_specs=(P(SEQ, RES, None), P(SEQ, RES, None)),
        check_vma=False,
    )
```

```python
import itertools
import math

import jax
import jax.numpy as jnp
import numpy as np
from jax import lax
from jax.experimental import pallas as pl
from jax.experimental.pallas import tpu as pltpu
from jax.sharding import Mesh, PartitionSpec as P

F32 = jnp.float32
BF16 = jnp.bfloat16

AXES = ("yl", "co", "yh", "zh", "zl", "x")
SIZES = (2, 2, 2, 2, 2, 4)
SEQ = ("yl", "co")
RES = ("yh", "zh", "zl", "x")
SWAPPED = ("yl", "co", "yh", "zh")
COLUMN = ("yh", "zh")
NEAR = ("zl", "x")

SEQS = 4
BLOCK = 64
ROWS = 512
WIDTH = 256
HEADS = 8
HEAD_DIM = 32
ALL_SEQS = 16
OUTER = 32
PAIR = 128
LEFT = ALL_SEQS * OUTER
FLAG_ROWS = 16
CHUNK = SEQS * BLOCK + FLAG_ROWS
MASKED = -1000000000.0
OTHER = -2000000000.0

FLIP = [(0, 1), (1, 0)]
NT = (((1,), (1,)), ((), ()))


def swap_pairs(flip):
    pairs = []
    for spot in np.ndindex(2, 2, 2, 2):
        target = (spot[2] ^ flip, spot[3], spot[0], spot[1])
        pairs.append(
            (int(np.ravel_multi_index(spot, (2, 2, 2, 2))), int(np.ravel_multi_index(target, (2, 2, 2, 2))))
        )
    return pairs


def swap(array, flip=0):
    return lax.ppermute(array, SWAPPED, swap_pairs(flip))


def shift(array, step, flip=0):
    return lax.ppermute(array, NEAR, [(z * 4 + i, (z ^ flip) * 4 + (i + step) % 4) for z in (0, 1) for i in range(4)])


def tie_body(*refs):
    pass


def tie(array, *first):
    anywhere = pl.BlockSpec(memory_space=pl.ANY)
    return pl.pallas_call(
        tie_body,
        in_specs=[anywhere] * (1 + len(first)),
        out_specs=anywhere,
        out_shape=jax.ShapeDtypeStruct(array.shape, array.dtype),
        input_output_aliases={0: 0},
        name="tie",
    )(array, *first)


def dot(a, b, dims=(((1,), (0,)), ((), ()))):
    return lax.dot_general(a, b, dims, preferred_element_type=F32)


def norm(data):
    centered = data - jnp.mean(data, axis=-1, keepdims=True)
    variance = jnp.mean(centered * centered, axis=-1, keepdims=True)
    return centered * lax.rsqrt(variance + 1e-05)


def iota(shape, dim):
    return lax.broadcasted_iota(jnp.int32, shape, dim)


def pack_body(block_ref, x_ref, filled_ref, flag_ref, out_ref):
    rows = SEQS * BLOCK
    out_ref[:rows, :] = x_ref[...]
    filled = filled_ref[...].astype(F32)
    block = block_ref[0]
    flags = flag_ref[pl.ds(block // 2, 1), :].astype(F32)
    live = filled * jnp.where(block % 2 == 0, flags[:, :BLOCK], flags[:, BLOCK:])
    lines = [jnp.concatenate([part[i : i + 1] for i in range(SEQS)], axis=1) for part in (filled, live)]
    lines.append(jnp.zeros((FLAG_ROWS - 2, WIDTH), F32))
    out_ref[rows:, :] = jnp.concatenate(lines, axis=0).astype(BF16)


def pack_chunk(block, lineup_state, lineup_filled, flags):
    vmem = pl.BlockSpec(memory_space=pltpu.VMEM)
    return pl.pallas_call(
        pack_body,
        in_specs=[pl.BlockSpec(memory_space=pltpu.SMEM), vmem, vmem, vmem],
        out_specs=vmem,
        out_shape=jax.ShapeDtypeStruct((CHUNK, WIDTH), BF16),
        name="pack_lineup",
    )(block, lineup_state.reshape(SEQS * BLOCK, WIDTH), lineup_filled, flags.reshape(-1, 2 * BLOCK))


def norm_body(x_ref, flipped_ref, after_ref, out_ref):
    rows = SEQS * BLOCK
    for slot, ref in enumerate((x_ref, flipped_ref)):
        out_ref[slot, :rows, :] = norm(ref[:rows, :].astype(F32)).astype(BF16)
        out_ref[slot, rows:, :] = ref[rows:, :]


def norm_chunks(chunk, flipped, after):
    vmem = pl.BlockSpec(memory_space=pltpu.VMEM)
    return pl.pallas_call(
        norm_body,
        in_specs=[vmem, vmem, pl.BlockSpec(memory_space=pl.ANY)],
        out_shape=jax.ShapeDtypeStruct((2, CHUNK, WIDTH), BF16),
        name="norm_lineup",
    )(chunk, flipped, after)


BIAS_STEP = 128
BIAS_PARTS = 1
GROUP = 32
COPIES = 4


def bias_body(pair_ref, weight_ref, *refs):
    out_ref, spread, normed = refs[-3:]

    @pl.when(pl.program_id(0) == 0)
    def _():
        wide = weight_ref[...]
        owner = iota((PAIR, WIDTH), 1) // HEADS

        def place(i, carry):
            spread[pl.ds(pl.multiple_of(i * PAIR, PAIR), PAIR), :] = jnp.where(
                owner == i, wide, jnp.zeros_like(wide)
            )
            return carry

        lax.fori_loop(0, GROUP, place, 0)

    groups = BIAS_STEP // GROUP
    cols = BLOCK // BIAS_PARTS
    ones = jnp.ones((PAIR, PAIR), BF16)

    def one(i, carry):
        for g in range(groups):
            raw = pair_ref[g * GROUP + i]
            centered = raw.astype(F32) - dot(raw, ones) * (1.0 / PAIR)
            variance = jnp.mean(centered * centered, axis=-1, keepdims=True)
            normed[g * cols : (g + 1) * cols, pl.ds(pl.multiple_of(i * PAIR, PAIR), PAIR)] = (
                centered * lax.rsqrt(variance + 1e-05)
            ).astype(BF16)
        return carry

    lax.fori_loop(0, GROUP, one, 0, unroll=8)
    result = dot(normed[...], spread[...]).astype(BF16)
    for g in range(groups):
        for c in range(COPIES):
            out_ref[c, g // 2, :, (g % 2) * WIDTH : (g % 2 + 1) * WIDTH] = result[g * cols : (g + 1) * cols]


def bias_blocks(couple_state, couple_offset_matrix, start, steps, *after):
    wide = jnp.tile(couple_offset_matrix, (1, GROUP))
    per_step = BIAS_STEP // BLOCK
    cols = BLOCK // BIAS_PARTS
    return pl.pallas_call(
        bias_body,
        grid=(steps,),
        in_specs=[
            pl.BlockSpec((BIAS_STEP, cols, PAIR), lambda i: (i + start, 0, 0)),
            pl.BlockSpec((PAIR, WIDTH), lambda i: (0, 0)),
        ]
        + [pl.BlockSpec(memory_space=pl.ANY)] * len(after),
        out_specs=pl.BlockSpec((COPIES, per_step, cols, BLOCK * HEADS), lambda i: (0, i + start, 0, 0)),
        out_shape=jax.ShapeDtypeStruct((COPIES, ROWS // BLOCK, cols, BLOCK * HEADS), BF16),
        scratch_shapes=[
            pltpu.VMEM((GROUP * PAIR, WIDTH), BF16),
            pltpu.VMEM((BIAS_STEP // GROUP * cols, GROUP * PAIR), BF16),
        ],
        compiler_params=pltpu.CompilerParams(vmem_limit_bytes=53 << 20),
        cost_estimate=pl.CostEstimate(flops=8 << 30, bytes_accessed=6 << 20, transcendentals=0),
        input_output_aliases={2: 0} if start else {},
        name="pair_bias",
    )(couple_state, wide, *after)


KEY_TILE = 512
KEYS = 2048
QH = BLOCK * HEADS
PER_TILE = KEY_TILE // BLOCK
SPOTS = [(zl, x, co) for co in (0, 1) for zl in (0, 1) for x in (0, 1, 3, 2)]


def key_body(*refs):
    parts, flags = refs[: len(SPOTS)], refs[len(SPOTS) : 2 * len(SPOTS)]
    wk_ref, wvt_ref, key_ref, value_ref, live_ref = refs[2 * len(SPOTS) :]

    @pl.when(pl.program_id(0) == 0)
    def _():
        lanes = jnp.concatenate([ref[...].astype(F32)[:, 1, :] for ref in flags], axis=0)
        live_ref[...] = jnp.concatenate([lanes, jnp.zeros((128 - 2 * len(SPOTS), WIDTH), F32)], axis=0).T

    for t in range(KEYS // KEY_TILE):
        blocks = [(b // 2, b % 2) for b in range(t * PER_TILE, (t + 1) * PER_TILE)]
        tile = jnp.concatenate([parts[i][slot] for i, slot in blocks], axis=0)
        lanes = slice(t * KEY_TILE, (t + 1) * KEY_TILE)
        key_ref[0, lanes, :] = dot(tile, wk_ref[...]).astype(BF16)
        value_ref[0, :, lanes] = dot(wvt_ref[...], tile, NT).astype(BF16)


def row_keys(parts, wk, wv):
    gathered = pl.BlockSpec((2, BLOCK, WIDTH), lambda s: (0, s, 0))
    masks = pl.BlockSpec((2, FLAG_ROWS, WIDTH), lambda s: (0, SEQS * BLOCK // FLAG_ROWS, 0))
    square = pl.BlockSpec((WIDTH, WIDTH), lambda s: (0, 0))
    return pl.pallas_call(
        key_body,
        grid=(SEQS,),
        in_specs=[*([gathered] * len(SPOTS)), *([masks] * len(SPOTS)), square, square],
        out_specs=[
            pl.BlockSpec((1, KEYS, WIDTH), lambda s: (s, 0, 0)),
            pl.BlockSpec((1, WIDTH, KEYS), lambda s: (s, 0, 0)),
            pl.BlockSpec((WIDTH, 128), lambda s: (0, 0)),
        ],
        out_shape=[
            jax.ShapeDtypeStruct((SEQS, KEYS, WIDTH), BF16),
            jax.ShapeDtypeStruct((SEQS, WIDTH, KEYS), BF16),
            jax.ShapeDtypeStruct((WIDTH, 128), F32),
        ],
        compiler_params=pltpu.CompilerParams(vmem_limit_bytes=57 << 20),
        cost_estimate=pl.CostEstimate(flops=4 << 30, bytes_accessed=12 << 20, transcendentals=0),
        name="row_keys",
    )(*parts, *parts, wk, wv.T)


def row_body(spot_ref, own_ref, x_ref, key_ref, value_ref, live, *refs):
    bias_refs = refs[:BIAS_PARTS]
    wq_ref, wg_ref, wo_ref, out_ref, *scratch = refs[BIAS_PARTS:]
    weights = scratch[-1]
    even, odd = scratch[0:2], scratch[2:4]
    step = pl.program_id(0)
    yl, core, zl, x = (spot_ref[i] for i in range(4))
    head_rows = (iota((BLOCK, HEADS, WIDTH), 2) // HEAD_DIM) == iota((BLOCK, HEADS, WIDTH), 1)

    def rows_of(s):
        return pl.ds(pl.multiple_of(s * BLOCK, BLOCK), BLOCK)

    def score(buffers):
        scores, highest = buffers
        rows = rows_of(step)
        queries = (dot(own_ref[0, rows, :], wq_ref[...]) * (1.0 / math.sqrt(HEAD_DIM))).astype(BF16).astype(F32)
        spread = (
            jnp.where(head_rows, jnp.broadcast_to(queries[:, None, :], (BLOCK, HEADS, WIDTH)), 0.0)
            .reshape(QH, WIDTH)
            .astype(BF16)
        )
        top = jnp.full((8, QH), -3e38, F32)
        mask_rows = live[rows, : 2 * len(SPOTS)]
        for t in range(KEYS // KEY_TILE):
            blocks = [(b // 2, b % 2) for b in range(t * PER_TILE, (t + 1) * PER_TILE)]
            lanes = slice(t * KEY_TILE, (t + 1) * KEY_TILE)
            bias = []
            for i, slot in blocks:
                flip, back, side = SPOTS[i]
                block = (yl ^ slot) * 16 + (core ^ side) * 8 + (zl ^ flip) * 4 + (x + 4 - back) % 4
                bias += [part[block] for part in bias_refs]
            product = dot(key_ref[0, lanes, :], spread, NT) + jnp.concatenate(bias, axis=0).astype(F32)
            alive = jnp.concatenate([mask_rows[:, 2 * i + slot : 2 * i + slot + 1] for i, slot in blocks], axis=0)
            product = jnp.where(alive > 0.0, product, MASKED)
            scores[lanes, :] = product
            top = jnp.maximum(top, jnp.max(product.reshape(KEY_TILE // 8, 8, QH), axis=0))
            yield
        highest[...] = jnp.broadcast_to(jnp.max(top, axis=0, keepdims=True), (8, QH))

    def attend(buffers):
        scores, highest = buffers
        rows = rows_of(step - 1)
        largest = highest[0:1, :]
        total = jnp.zeros((8, QH), F32)
        for t in range(KEYS // KEY_TILE):
            lanes = slice(t * KEY_TILE, (t + 1) * KEY_TILE)
            expo = jnp.exp(scores[lanes, :] - largest)
            total = total + jnp.sum(expo.reshape(KEY_TILE // 8, 8, QH), axis=0)
            weights[lanes, :] = expo.astype(BF16)
            yield
        mixed = dot(value_ref[0], weights[...])
        mixed = mixed / jnp.sum(total, axis=0, keepdims=True)
        picked = jnp.where(head_rows, mixed.T.reshape(BLOCK, HEADS, WIDTH), 0.0)
        attended = jnp.sum(picked, axis=1)
        gate = jax.nn.sigmoid(dot(own_ref[0, rows, :], wg_ref[...]))
        added = dot((gate * attended).astype(BF16), wo_ref[...])
        out_ref[rows, :] = (x_ref[rows, :].astype(F32) + added).astype(BF16)

    def run(*work):
        for _ in itertools.zip_longest(*work):
            pass

    @pl.when(step == 0)
    def _():
        out_ref[SEQS * BLOCK :, :] = x_ref[SEQS * BLOCK :, :]
        run(score(even))

    @pl.when(step % 2 == 1)
    def _():
        run(score(odd), attend(even))

    @pl.when(step == 2)
    def _():
        run(score(even), attend(odd))

    @pl.when(step == SEQS)
    def _():
        run(attend(odd))


def row_attention(spot, own, x, keys, values, live, biases, wq, wg, wo):
    whole = lambda shape: pl.BlockSpec(shape, lambda s: (0,) * len(shape))
    square = whole((WIDTH, WIDTH))
    return pl.pallas_call(
        row_body,
        grid=(SEQS + 1,),
        in_specs=[
            pl.BlockSpec(memory_space=pltpu.SMEM),
            whole((2, CHUNK, WIDTH)),
            whole((CHUNK, WIDTH)),
            pl.BlockSpec((1, KEYS, WIDTH), lambda s: (jnp.minimum(s, SEQS - 1), 0, 0)),
            pl.BlockSpec((1, WIDTH, KEYS), lambda s: (jnp.maximum(s - 1, 0), 0, 0)),
            whole((WIDTH, 128)),
            *([whole((KEYS // BLOCK, BLOCK // BIAS_PARTS, QH))] * BIAS_PARTS),
            square,
            square,
            square,
        ],
        out_specs=whole((CHUNK, WIDTH)),
        out_shape=jax.ShapeDtypeStruct((CHUNK, WIDTH), BF16),
        scratch_shapes=[
            *([pltpu.VMEM((KEYS, QH), F32), pltpu.VMEM((8, QH), F32)] * 2),
            pltpu.VMEM((KEYS, QH), BF16),
        ],
        compiler_params=pltpu.CompilerParams(vmem_limit_bytes=57 << 20),
        cost_estimate=pl.CostEstimate(flops=12 << 30, bytes_accessed=12 << 20, transcendentals=4 << 20),
        name="row_attention",
    )(spot, own, x, keys, values, live, *biases, wq, wg, wo)


PART = 16
PART_ROWS = ALL_SEQS * PART
BACK = SEQS * BLOCK + 3 * BLOCK
SIDE = LEFT + 128


def column_body(
    mine_ref, x0_ref, x3_ref, x2_ref, x1_ref, w_ref, wo_ref, left_ref, right_ref, out_ref, a_ref, masks,
):
    x_refs = (x0_ref, x1_ref, x2_ref, x3_ref)
    mine = mine_ref[0]
    for b in range(4):
        lanes = x_refs[b][SEQS * BLOCK :, :].astype(F32)
        masks[:, b * 128 : b * 128 + FLAG_ROWS] = lanes.T
    one_row = iota((PART_ROWS, PART_ROWS), 0)
    one_col = iota((PART_ROWS, PART_ROWS), 1)
    same = (one_row % PART) == (one_col % PART)

    def sequence(shape):
        slot = iota(shape, 0) // PART
        return ((slot // SEQS) ^ mine) * SEQS + slot % SEQS

    keep = iota((PART_ROWS, LEFT), 1) % ALL_SEQS == sequence((PART_ROWS, LEFT))
    keep_flag = iota((PART_ROWS, 128), 1) == sequence((PART_ROWS, 128))
    lane_head = iota((PART_ROWS, WIDTH), 1) // HEAD_DIM
    for g in range(BLOCK // PART):
        spots = [(s // SEQS, (s % SEQS) * BLOCK + g * PART) for s in range(ALL_SEQS)]
        data = jnp.concatenate([x_refs[b][r : r + PART, :] for b, r in spots], axis=0).astype(F32)
        filled = jnp.concatenate([masks[r : r + PART, b * 128 : b * 128 + 1] for b, r in spots], axis=0)
        live = jnp.concatenate([masks[r : r + PART, b * 128 + 1 : b * 128 + 2] for b, r in spots], axis=0)
        filled_lane = jnp.broadcast_to(filled, (PART_ROWS, 128)).T[0:1, :]
        fill = jnp.where(same, MASKED, OTHER)
        use = jnp.logical_and(same, jnp.broadcast_to(filled_lane, (PART_ROWS, PART_ROWS)) > 0.0)
        line = dot(norm(data).astype(BF16), w_ref[...])
        queries = (line[:, :WIDTH] * (1.0 / math.sqrt(HEAD_DIM))).astype(BF16)
        keys = line[:, WIDTH : 2 * WIDTH].astype(BF16)
        value = line[:, 2 * WIDTH : 3 * WIDTH].astype(BF16)
        gate = jax.nn.sigmoid(line[:, 3 * WIDTH :])
        mixed = jnp.zeros((PART_ROWS, WIDTH), F32)
        for h in range(HEADS):
            head = lane_head == h
            product = dot(jnp.where(head, queries, jnp.zeros_like(queries)), keys, NT)
            product = jnp.where(use, product, fill)
            expo = jnp.exp(product - jnp.max(product, axis=1, keepdims=True))
            total = jnp.sum(expo, axis=1, keepdims=True)
            mixed = mixed + jnp.where(head, dot(expo.astype(BF16), value) / total, 0.0)
        result = (data + dot((gate * mixed).astype(BF16), wo_ref[...])).astype(BF16)
        for s in range(SEQS):
            out_ref[s * BLOCK + g * PART : s * BLOCK + (g + 1) * PART, :] = result[s * PART : (s + 1) * PART]
        normed = norm(result.astype(F32)).astype(BF16)
        flags = jnp.where(keep_flag, jnp.broadcast_to(live, (PART_ROWS, 128)), 0.0)
        flags = jnp.sum(flags.reshape(ALL_SEQS, PART, 128), axis=0).astype(BF16)
        for weight_ref, out in ((right_ref, out_ref), (left_ref, a_ref)):
            wide = (dot(normed, weight_ref[...]) * live).astype(BF16).astype(F32)
            wide = jnp.where(keep, wide, 0.0)
            wide = jnp.sum(wide.reshape(ALL_SEQS, PART, LEFT), axis=0).astype(BF16)
            rows = slice(g * PART, (g + 1) * PART)
            if out is out_ref:
                first = SEQS * BLOCK + g * PART
                out[first : first + PART, :] = wide[:, :WIDTH]
                out[first + BLOCK : first + BLOCK + PART, :] = wide[:, WIDTH:]
                out[first + 2 * BLOCK : first + 2 * BLOCK + PART, :128] = flags
                out[first + 2 * BLOCK : first + 2 * BLOCK + PART, 128:] = flags
            else:
                for k in range(out.shape[0]):
                    out[k, rows, :LEFT] = wide
                    out[k, rows, LEFT:] = flags


def column_attention(mine, rows, query_matrix, final_matrix, side_matrix):
    left = jnp.repeat(side_matrix[:, :OUTER], ALL_SEQS, axis=1)
    right = jnp.repeat(side_matrix[:, OUTER:], ALL_SEQS, axis=1)
    vmem = pl.BlockSpec(memory_space=pltpu.VMEM)
    return pl.pallas_call(
        column_body,
        in_specs=[pl.BlockSpec(memory_space=pltpu.SMEM)] + [vmem] * 8,
        out_specs=[vmem] * 2,
        out_shape=[
            jax.ShapeDtypeStruct((BACK, WIDTH), BF16),
            jax.ShapeDtypeStruct((8, BLOCK, SIDE), BF16),
        ],
        scratch_shapes=[pltpu.VMEM((WIDTH, 512), F32)],
        compiler_params=pltpu.CompilerParams(vmem_limit_bytes=24 << 20),
        cost_estimate=pl.CostEstimate(flops=4 << 30, bytes_accessed=3 << 20, transcendentals=2 << 20),
        name="column_attention",
    )(mine, *rows, query_matrix, final_matrix, left, right)


PAIR_STEP = 128
WIDE = BLOCK * PAIR
STRIDE = BLOCK + 8


def pair_body(a_ref, b_ref, w_ref, pair_ref, out_ref, aligned_ref, table, even, odd):
    step = pl.program_id(0)
    steps = ROWS // PAIR_STEP
    per_dot = 4

    def multiply(update):
        left = a_ref[:, :LEFT]
        count = dot(a_ref[:, LEFT:], b_ref[BACK - BLOCK :, :128], NT)
        scale = 1.0 / jnp.maximum(count, 1.0)
        for j in range(0, BLOCK, per_dot):
            part = dot(left, table[:, j * PAIR : (j + per_dot) * PAIR])
            for d in range(per_dot):
                update[pl.ds(j + d, PAIR_STEP, stride=STRIDE), :] = (
                    part[:, d * PAIR : (d + 1) * PAIR] * scale[:, j + d : j + d + 1]
                )
            yield

    def finish(update):
        share = PAIR_STEP * per_dot // BLOCK
        for first in range(0, PAIR_STEP, share):
            for i in range(first, first + share):
                rows = update[i * STRIDE : i * STRIDE + BLOCK, :]
                out_ref[i] = (pair_ref[i].astype(F32) + rows).astype(BF16)
            yield

    def run(*work):
        for _ in itertools.zip_longest(*work):
            pass

    @pl.when(step == 0)
    def _():
        aligned_ref[...] = b_ref[: SEQS * BLOCK, :]
        keep = (iota((16 * ALL_SEQS, LEFT), 1) % ALL_SEQS) == (iota((16 * ALL_SEQS, LEFT), 0) % ALL_SEQS)
        fold = (iota((LEFT, 128), 0) // ALL_SEQS == iota((LEFT, 128), 1)).astype(BF16)

        def build(q, carry):
            first = pl.multiple_of(SEQS * BLOCK + q * 16, 16)
            rows = jnp.concatenate(
                [b_ref[pl.ds(first, 16), :], b_ref[pl.ds(pl.multiple_of(first + BLOCK, 16), 16), :]], axis=1
            ).astype(F32)
            rows = jnp.broadcast_to(rows[:, None, :], (16, ALL_SEQS, LEFT)).reshape(16 * ALL_SEQS, LEFT)
            right = dot(jnp.where(keep, rows, 0.0).astype(BF16), fold).astype(BF16)
            for c in range(OUTER // 2):
                part = dot(right, w_ref[:, c * 256 : (c + 1) * 256]).astype(BF16)
                for j in range(16):
                    lanes = pl.ds(pl.multiple_of((q * 16 + j) * PAIR, PAIR), PAIR)
                    for d in range(2):
                        table[(2 * c + d) * 16 : (2 * c + d + 1) * 16, lanes] = part[
                            j * 16 : (j + 1) * 16, d * PAIR : (d + 1) * PAIR
                        ]
            return carry

        lax.fori_loop(0, BLOCK // 16, build, 0)
        run(multiply(even))

    @pl.when(step % 2 == 1)
    def _():
        run(multiply(odd), finish(even))

    @pl.when(jnp.logical_and(step > 0, jnp.logical_and(step % 2 == 0, step < steps)))
    def _():
        run(multiply(even), finish(odd))

    @pl.when(step == steps)
    def _():
        run(finish(odd))


def pair_update(left, right, final_matrix, couple_state):
    wide = final_matrix.reshape(OUTER, OUTER, PAIR).transpose(1, 0, 2).reshape(OUTER, OUTER * PAIR)
    wide = jnp.pad(wide, ((0, 128 - OUTER), (0, 0)))
    steps = ROWS // PAIR_STEP
    block = pl.BlockSpec((PAIR_STEP, BLOCK, PAIR), lambda i: (jnp.maximum(i - 1, 0), 0, 0))
    return pl.pallas_call(
        pair_body,
        grid=(steps + 1,),
        in_specs=[
            pl.BlockSpec((PAIR_STEP, SIDE), lambda i: (jnp.minimum(i, steps - 1), 0)),
            pl.BlockSpec((BACK, WIDTH), lambda i: (0, 0)),
            pl.BlockSpec((128, OUTER * PAIR), lambda i: (0, 0)),
            block,
        ],
        out_specs=[block, pl.BlockSpec((SEQS * BLOCK, WIDTH), lambda i: (0, 0))],
        out_shape=[
            jax.ShapeDtypeStruct(couple_state.shape, BF16),
            jax.ShapeDtypeStruct((SEQS * BLOCK, WIDTH), BF16),
        ],
        scratch_shapes=[
            pltpu.VMEM((LEFT, WIDE), BF16),
            pltpu.VMEM((STRIDE * PAIR_STEP, PAIR), F32),
            pltpu.VMEM((STRIDE * PAIR_STEP, PAIR), F32),
        ],
        compiler_params=pltpu.CompilerParams(vmem_limit_bytes=57 << 20),
        cost_estimate=pl.CostEstimate(flops=8 << 30, bytes_accessed=18 << 20, transcendentals=0),
        name="pair_update",
    )(left, right, wide, couple_state)


def per_device(
    lineup_state,
    couple_state,
    lineup_filled,
    observed_amino_flag,
    horizontal_query_matrix,
    horizontal_final_matrix,
    couple_offset_matrix,
    vertical_query_matrix,
    vertical_final_matrix,
    tensor_mean_side_matrix,
    tensor_mean_final_matrix,
):
    spot = jnp.stack([lax.axis_index(axis) for axis in ("yl", "co", "zl", "x")]).astype(jnp.int32)
    block = lax.axis_index(RES).astype(jnp.int32).reshape(1)
    mine = (lax.axis_index("yh") * 2 + lax.axis_index("zh")).astype(jnp.int32).reshape(1)
    packed = pack_chunk(block, lineup_state, lineup_filled, observed_amino_flag)
    chunk = swap(packed)
    send = bias_blocks(couple_state, couple_offset_matrix, 0, 1)
    kept = norm_chunks(chunk, swap(packed, 1), send)
    parts = []
    for flip in (0, 1):
        part = shift(kept, 0, 1) if flip else kept
        parts += [part, shift(kept, 1, flip), shift(kept, -1, flip)]
    send = bias_blocks(couple_state, couple_offset_matrix, 1, 2, send, kept)
    send = bias_blocks(couple_state, couple_offset_matrix, 3, 1, send, *parts[1:])
    parts = parts[:3] + [shift(parts[1], 1)] + parts[3:] + [shift(parts[5], -1)]
    send = tie(send, parts[3], parts[7])
    parts += [lax.ppermute(part, "co", FLIP) for part in parts]
    biases = [lax.all_to_all(send.reshape((32,) + send.shape[2:]), RES, 0, 0)]
    wq, wk, wv, wg = (horizontal_query_matrix[:, i * WIDTH : (i + 1) * WIDTH] for i in range(4))
    keys, values, live = row_keys(parts, wk, wv)
    rows = row_attention(spot, kept, chunk, keys, values, live, biases, wq, wg, horizontal_final_matrix)
    rows = [rows] + [lax.ppermute(rows, COLUMN, [(i, i ^ k) for i in range(4)]) for k in (3, 2, 1)]
    back, left = column_attention(
        mine, rows, vertical_query_matrix, vertical_final_matrix, tensor_mean_side_matrix
    )
    back = swap(back)
    left = lax.all_to_all(left, NEAR, 0, 0)
    pair, aligned = pair_update(left.reshape(ROWS, SIDE), back, tensor_mean_final_matrix, couple_state)
    return aligned.reshape(SEQS, BLOCK, WIDTH), pair


def solution(mesh):
    fine = Mesh(mesh.devices.reshape(SIZES), AXES)
    return jax.shard_map(
        per_device,
        mesh=fine,
        in_specs=(
            P(SEQ, RES, None),
            P(SEQ, RES, None),
            P(SEQ, RES),
            P(),
            P(),
            P(),
            P(),
            P(),
            P(),
            P(),
            P(),
        ),
        out_specs=(P(SEQ, RES, None), P(SEQ, RES, None)),
        check_vma=False,
    )
```
